256 devices in a mesh: az: 32 (over y, x, z_lo), rad: 8 (over z_hi, core).
Axes of the slice: x: 4, y: 4, z: 8 (z_hi: 4, z_lo: 2; z = z_hi * 2 + z_lo), core: 2. Of those that a mesh axis runs over, the one named last changes fastest.
Arguments:
- state: float32 [8, 32, 64, 4096], P(None, 'rad', None, 'az'), may hold values from -6 to 6
- shifts: int32 [32], P('rad'), may hold values from 0 to 4095
- fracs: float32 [32], P('rad'), may hold values from 0 to 1
Outputs:
- advanced: float32 [8, 32, 64, 4096], P(None, 'rad', None, 'az')
The draws below stay inside these ranges and needn't reach their ends.
All inputs are finite; a program needn't handle non-finite values.
Results may differ from the reference program's by a relative error of at most 0.00002.
Values sent between devices are 32-bit elements; how exact they have to be, the bound alone decides.
No kernel may reach another device: no remote copies, remote signals or barrier semaphores. Data moves between devices by JAX's collectives and lax.ppermute only.
A program may use at most 128 MiB of HBM per device.

```python
import jax
import jax.numpy as jnp
from jax import lax

Z = 64
NVAR = 8
NR = 32
NA = 4096


def plant(entries, key, smallest, top_value):
    longest = entries.shape.index(max(entries.shape))
    spots = []
    for shift in (0, 1):
        where = [jax.random.randint(jax.random.fold_in(key, axis), (), 0, length) for axis, length in enumerate(entries.shape)]
        where[longest] = (where[longest] + shift) % entries.shape[longest]
        spots.append(tuple(where))
    return entries.at[spots[0]].set(smallest).at[spots[1]].set(top_value)


def block_levels(key, extent, pieces, low, high):
    loudness, own = 1.0, jax.random.fold_in(key, 6)
    for axis_at, parts in pieces:
        draws = jnp.exp(jax.random.uniform(jax.random.fold_in(own, axis_at), (parts,), jnp.float32, low / len(pieces), high / len(pieces)))
        loudness = loudness * jnp.repeat(draws, extent[axis_at] // parts).reshape([-1 if axis == axis_at else 1 for axis in range(len(extent))])
    return loudness


def noise(rng, dims, deviation, bound, shards=(), kind=jnp.bfloat16):
    values = jax.random.normal(rng, dims, jnp.float32) * deviation
    if len(shards) > 0:
        values = block_levels(rng, dims, shards, -0.22, 0.18) * values
    return jnp.clip(values, min=-bound, max=bound).astype(kind)


def setup_inputs(seed: int = 0) -> dict:
    splits = jax.random.split(jax.random.key(seed), 4)
    state = noise(splits[0], (NVAR, NR, Z, NA), 1.0, 6.0, ((1, 8), (3, 32)), jnp.float32)
    shifts = plant(jax.random.randint(splits[1], (NR,), 0, NA), jax.random.fold_in(splits[1], 1), 0, NA - 1).astype(jnp.int32)
    fracs = jnp.clip(1.0 * jax.random.uniform(splits[2], (NR,), jnp.float32) ** block_levels(splits[2], (NR,), ((0, 8),), -0.2, 0.2), 0.0, 1.0)
    return {"state": state, "shifts": shifts, "fracs": fracs}


def fields(S):
    rho, vx, vy, vz, bx, by, bz, ent = [S[i] for i in range(8)]
    return jnp.stack([vy * bz - vz * by, vz * bx - vx * bz, vx * by - vy * bx,
                      rho * vx, rho * vy, rho * vz, ent,
                      0.5 * (bx * bx + by * by + bz * bz)])


def advance(center, xplus, xminus, yplus, yminus, coord_x, coord_z):
    dxf = 0.5 * (fields(xplus) - fields(xminus))
    dyf = 0.5 * (fields(yplus) - fields(yminus))
    fc = fields(center)
    fpad = jnp.pad(fc, ((0, 0), (0, 0), (1, 1), (0, 0)))
    dzf = 0.5 * (fpad[:, :, 2:] - fpad[:, :, :-2])
    rho, vx, vy, vz, bx, by, bz, ent = [center[i] for i in range(8)]
    rates = jnp.stack([
        -(dxf[3] + dyf[4] + dzf[5]),
        2.0 * vy + 3.0 * coord_x - dxf[7],
        -0.5 * vx - dyf[7],
        -coord_z - dzf[7],
        dyf[2] - dzf[1],
        dzf[0] - dxf[2],
        dxf[1] - dyf[0],
        -(vx * dxf[6] + vy * dyf[6] + vz * dzf[6])])
    return center + 0.2 * rates


def reference(state, shifts, fracs):
    def one_radius(item):
        row, step, frac = item
        return (1.0 - frac) * jnp.roll(row, step, axis=2) + frac * jnp.roll(row, step + 1, axis=2)

    moved = lax.map(one_radius, (jnp.moveaxis(state, 1, 0), shifts, fracs))
    remapped = jnp.moveaxis(moved, 0, 1)
    zero = jnp.zeros_like(remapped[:, :1])
    xplus = jnp.concatenate([remapped[:, 1:], zero], axis=1)
    xminus = jnp.concatenate([zero, remapped[:, :-1]], axis=1)
    yplus = jnp.roll(remapped, -1, axis=3)
    yminus = jnp.roll(remapped, 1, axis=3)
    coord_x = ((jnp.arange(NR, dtype=jnp.float32) + 0.5) / NR - 0.5)[:, None, None]
    coord_z = ((jnp.arange(Z, dtype=jnp.float32) + 0.5) / Z - 0.5)[None, :, None]
    return advance(remapped, xplus, xminus, yplus, yminus, coord_x, coord_z)
```

```python
import jax
import jax.numpy as jnp
from jax import lax
from jax.experimental import pallas as pl
from jax.experimental.pallas import tpu as pltpu
from jax.sharding import PartitionSpec as P

F32 = jnp.float32
VMEM = pl.BlockSpec(memory_space=pltpu.VMEM)
SMEM = pl.BlockSpec(memory_space=pltpu.SMEM)


def remap_kernel(steps_ref, frac_ref, x_ref, o_ref):
    blocks, height, width = x_ref.shape
    block_shift = steps_ref[0]
    lane_shift = steps_ref[1]
    frac = frac_ref[0]
    lane = lax.broadcasted_iota(jnp.int32, (height, width), 1)
    own = lane + lane_shift < width
    own_next = lane + lane_shift + 1 < width
    ends = jnp.zeros((height, width), F32)
    for i in range(blocks):
        near = x_ref[lax.rem(i - block_shift + 2 * blocks, blocks)]
        far = x_ref[lax.rem(i - block_shift - 1 + 2 * blocks, blocks)]
        first = pltpu.roll(jnp.where(own, near, far), lane_shift, 1)
        second = pltpu.roll(jnp.where(own_next, near, far), lane_shift + 1, 1)
        cells = (1.0 - frac) * first + frac * second
        o_ref[i, :height, :] = cells
        turned = pltpu.roll(cells, (2 * i + 1) % width, 1)
        ends = jnp.where(lane // 2 == i, turned, ends)
    rows = jnp.transpose(jnp.concatenate([ends, jnp.zeros_like(ends)], axis=0))
    for i in range(blocks):
        last = 2 * ((i - 1) % blocks)
        head = 2 * ((i + 1) % blocks) + 1
        o_ref[i, height : height + 1, :] = rows[last : last + 1]
        o_ref[i, height + 1 : height + 2, :] = rows[head : head + 1]


def products(S):
    rho, vx, vy, vz, bx, by, bz, ent = S
    return (
        vy * bz - vz * by,
        vz * bx - vx * bz,
        vx * by - vy * bx,
        rho * vx,
        rho * vy,
        rho * vz,
        ent,
        0.5 * (bx * bx + by * by + bz * bz),
    )


def edge_kernel(s_ref, low_ref, high_ref):
    radii = s_ref.shape[1]
    height = low_ref.shape[1]
    for r, out in ((0, low_ref), (radii - 1, high_ref)):
        wx, wy, wz, fx, fy, fz, es, pm = products([s_ref[v, r, :height] for v in range(8)])
        for at, field in enumerate((wy, wz, fx, es, pm)):
            out[at] = field


def update_kernel(first_ref, s_ref, below_ref, above_ref, o_ref, f_ref):
    radii = s_ref.shape[1]
    height, width = o_ref.shape[2:]
    total_radii = first_ref[1]
    pad = 8
    lane = lax.broadcasted_iota(jnp.int32, (height, width), 1)
    level = lax.broadcasted_iota(jnp.int32, (height, width), 0)
    zk = (level.astype(F32) + 0.5) / height - 0.5
    for r in range(radii):
        for at, field in enumerate(products([s_ref[v, r, :height] for v in range(8)])):
            f_ref[at, r, pad : pad + height] = field
            f_ref[at, r, :pad] = jnp.zeros((pad, width), F32)
            f_ref[at, r, pad + height :] = jnp.zeros((pad, width), F32)
    sides = [
        jnp.concatenate([s_ref[v, r, height : height + 2] for r in range(radii)], axis=0)
        for v in range(8)
    ]
    wx, wy, wz, fx, fy, fz, es, pm = products(sides)
    rows = jnp.concatenate([wx, wz, fy, es, pm], axis=0)
    used = rows.shape[0]
    columns = jnp.transpose(
        jnp.concatenate([rows, jnp.zeros((width - used, width), F32)], axis=0)
    )[:height]
    spot = {0: 0, 2: 1, 4: 2, 6: 3, 7: 4}

    for r in range(radii):
        rho, vx, vy, vz, bx, by, bz, ent = [s_ref[v, r, :height] for v in range(8)]
        xr = ((first_ref[0] + r).astype(F32) + 0.5) / total_radii.astype(F32) - 0.5
        place = {1: 0, 2: 1, 3: 2, 6: 3, 7: 4}

        def dx(at):
            plus = above_ref[place[at]] if r == radii - 1 else f_ref[at, r + 1, pad : pad + height]
            minus = below_ref[place[at]] if r == 0 else f_ref[at, r - 1, pad : pad + height]
            return 0.5 * (plus - minus)

        def dy(at):
            here = f_ref[at, r, pad : pad + height]
            col = spot[at] * 2 * radii + 2 * r
            left = columns[:, col : col + 1]
            right = columns[:, col + 1 : col + 2]
            plus = jnp.where(lane == width - 1, right, pltpu.roll(here, width - 1, 1))
            minus = jnp.where(lane == 0, left, pltpu.roll(here, 1, 1))
            return 0.5 * (plus - minus)

        def dz(at):
            plus = f_ref[at, r, pad + 1 : pad + 1 + height]
            minus = f_ref[at, r, pad - 1 : pad - 1 + height]
            return 0.5 * (plus - minus)

        o_ref[0, r] = rho + 0.2 * -(dx(3) + dy(4) + dz(5))
        o_ref[1, r] = vx + 0.2 * (2.0 * vy + 3.0 * xr - dx(7))
        o_ref[2, r] = vy + 0.2 * (-0.5 * vx - dy(7))
        o_ref[3, r] = vz + 0.2 * (-zk - dz(7))
        o_ref[4, r] = bx + 0.2 * (dy(2) - dz(1))
        o_ref[5, r] = by + 0.2 * (dz(0) - dx(2))
        o_ref[6, r] = bz + 0.2 * (dx(1) - dy(0))
        o_ref[7, r] = ent + 0.2 * -(vx * dx(6) + vy * dy(6) + vz * dz(6))


def on_device(state, shifts, fracs):
    variables, radii, height, width = state.shape
    count = variables * radii
    bands = lax.axis_size("rad")
    band = lax.axis_index("rad")
    turned = lax.all_to_all(state.reshape(count, height, width), "az", 0, 0, tiled=True)
    mine = lax.axis_index("az") % radii
    shift = lax.dynamic_index_in_dim(shifts, mine, keepdims=False)
    frac = lax.dynamic_slice_in_dim(fracs, mine, 1)
    steps = jnp.stack([shift // width, shift % width])
    moved = pl.pallas_call(
        remap_kernel,
        out_shape=jax.ShapeDtypeStruct((count, height + 8, width), F32),
        in_specs=[SMEM, SMEM, VMEM],
        out_specs=VMEM,
        name="remap",
    )(steps, frac, turned)
    remapped = lax.all_to_all(moved, "az", 0, 0, tiled=True).reshape(
        variables, radii, height + 8, width
    )
    edge = jax.ShapeDtypeStruct((5, height, width), F32)
    low, high = pl.pallas_call(
        edge_kernel, out_shape=(edge, edge), in_specs=[VMEM], out_specs=(VMEM, VMEM), name="edges"
    )(remapped)
    below = lax.ppermute(high, "rad", [(i, i + 1) for i in range(bands - 1)])
    above = lax.ppermute(low, "rad", [(i + 1, i) for i in range(bands - 1)])
    places = jnp.stack([band * radii, bands * radii]).astype(jnp.int32)
    return pl.pallas_call(
        update_kernel,
        out_shape=jax.ShapeDtypeStruct(state.shape, F32),
        in_specs=[SMEM, VMEM, VMEM, VMEM],
        out_specs=VMEM,
        scratch_shapes=[pltpu.VMEM((8, radii, height + 16, width), F32)],
        compiler_params=pltpu.CompilerParams(vmem_limit_bytes=32 * 2**20),
        name="update",
    )(places, remapped, below, above)


def solution(mesh):
    in_specs = (P(None, "rad", None, "az"), P("rad"), P("rad"))
    out_specs = P(None, "rad", None, "az")
    return jax.shard_map(
        on_device, mesh=mesh, in_specs=in_specs, out_specs=out_specs, check_vma=False
    )
```

```python
import jax
import jax.numpy as jnp
from jax import lax
from jax.experimental import pallas as pl
from jax.experimental.pallas import tpu as pltpu
from jax.sharding import PartitionSpec as P

F32 = jnp.float32
VMEM = pl.BlockSpec(memory_space=pltpu.VMEM)
SMEM = pl.BlockSpec(memory_space=pltpu.SMEM)
GRANT = pltpu.CompilerParams(vmem_limit_bytes=16 * 2**20)


def remap_kernel(shifts_ref, fracs_ref, x_ref, o_ref):
    blocks, height, width = x_ref.shape
    mine = lax.rem(lax.axis_index("az"), shifts_ref.shape[0])
    shift = shifts_ref[mine]
    frac = fracs_ref[mine]
    block_shift = lax.div(shift, width)
    lane_shift = lax.rem(shift, width)
    lane = lax.broadcasted_iota(jnp.int32, (height, width), 1)
    own = lane + lane_shift < width
    own_next = lane + lane_shift + 1 < width
    ends = jnp.zeros((height, width), F32)
    for i in range(blocks):
        near = x_ref[lax.rem(i - block_shift + 2 * blocks, blocks)]
        far = x_ref[lax.rem(i - block_shift - 1 + 2 * blocks, blocks)]
        first = pltpu.roll(jnp.where(own, near, far), lane_shift, 1)
        second = pltpu.roll(jnp.where(own_next, near, far), lane_shift + 1, 1)
        cells = (1.0 - frac) * first + frac * second
        o_ref[i, :height, :] = cells
        turned = pltpu.roll(cells, (2 * i + 1) % width, 1)
        ends = jnp.where(lane // 2 == i, turned, ends)
    rows = jnp.transpose(jnp.concatenate([ends, jnp.zeros_like(ends)], axis=0))
    for i in range(blocks):
        last = 2 * ((i - 1) % blocks)
        head = 2 * ((i + 1) % blocks) + 1
        o_ref[i, height : height + 1, :] = rows[last : last + 1]
        o_ref[i, height + 1 : height + 2, :] = rows[head : head + 1]


def products(S):
    rho, vx, vy, vz, bx, by, bz, ent = S
    return (
        vy * bz - vz * by,
        vz * bx - vx * bz,
        vx * by - vy * bx,
        rho * vx,
        rho * vy,
        rho * vz,
        ent,
        0.5 * (bx * bx + by * by + bz * bz),
    )


def edge_kernel(s_ref, chip_ref, far_ref):
    radii = s_ref.shape[1]
    height = chip_ref.shape[1]
    odd = lax.rem(lax.axis_index("rad"), 2)
    for r, out in ((jnp.where(odd == 1, 0, radii - 1), chip_ref), (jnp.where(odd == 1, radii - 1, 0), far_ref)):
        wx, wy, wz, fx, fy, fz, es, pm = products([s_ref[v, r, :height] for v in range(8)])
        for at, field in enumerate((wy, wz, fx, es, pm)):
            out[at] = field


def update_kernel(s_ref, chip_ref, far_ref, o_ref, f_ref):
    radii = s_ref.shape[1]
    height, width = o_ref.shape[2:]
    bands = lax.axis_size("rad")
    band = lax.axis_index("rad")
    odd = lax.rem(band, 2) == 1
    total_radii = radii * bands
    pad = 8
    lane = lax.broadcasted_iota(jnp.int32, (height, width), 1)
    level = lax.broadcasted_iota(jnp.int32, (height, width), 0)
    zk = (level.astype(F32) + 0.5) / height - 0.5
    for r in range(radii):
        for at, field in enumerate(products([s_ref[v, r, :height] for v in range(8)])):
            f_ref[at, r, pad : pad + height] = field
            f_ref[at, r, :pad] = jnp.zeros((pad, width), F32)
            f_ref[at, r, pad + height :] = jnp.zeros((pad, width), F32)
    sides = [
        jnp.concatenate([s_ref[v, r, height : height + 2] for r in range(radii)], axis=0)
        for v in range(8)
    ]
    wx, wy, wz, fx, fy, fz, es, pm = products(sides)
    rows = jnp.concatenate([wx, wz, fy, es, pm], axis=0)
    used = rows.shape[0]
    columns = jnp.transpose(
        jnp.concatenate([rows, jnp.zeros((width - used, width), F32)], axis=0)
    )[:height]
    spot = {0: 0, 2: 1, 4: 2, 6: 3, 7: 4}
    place = {1: 0, 2: 1, 3: 2, 6: 3, 7: 4}

    for r in range(radii):
        rho, vx, vy, vz, bx, by, bz, ent = [s_ref[v, r, :height] for v in range(8)]
        xr = ((band * radii + r).astype(F32) + 0.5) / total_radii - 0.5

        def dx(at):
            if r == radii - 1:
                plus = jnp.where(odd, far_ref[place[at]], chip_ref[place[at]])
            else:
                plus = f_ref[at, r + 1, pad : pad + height]
            if r == 0:
                minus = jnp.where(odd, chip_ref[place[at]], far_ref[place[at]])
            else:
                minus = f_ref[at, r - 1, pad : pad + height]
            return 0.5 * (plus - minus)

        def dy(at):
            here = f_ref[at, r, pad : pad + height]
            col = spot[at] * 2 * radii + 2 * r
            left = columns[:, col : col + 1]
            right = columns[:, col + 1 : col + 2]
            plus = jnp.where(lane == width - 1, right, pltpu.roll(here, width - 1, 1))
            minus = jnp.where(lane == 0, left, pltpu.roll(here, 1, 1))
            return 0.5 * (plus - minus)

        def dz(at):
            plus = f_ref[at, r, pad + 1 : pad + 1 + height]
            minus = f_ref[at, r, pad - 1 : pad - 1 + height]
            return 0.5 * (plus - minus)

        o_ref[0, r] = rho + 0.2 * -(dx(3) + dy(4) + dz(5))
        o_ref[1, r] = vx + 0.2 * (2.0 * vy + 3.0 * xr - dx(7))
        o_ref[2, r] = vy + 0.2 * (-0.5 * vx - dy(7))
        o_ref[3, r] = vz + 0.2 * (-zk - dz(7))
        o_ref[4, r] = bx + 0.2 * (dy(2) - dz(1))
        o_ref[5, r] = by + 0.2 * (dz(0) - dx(2))
        o_ref[6, r] = bz + 0.2 * (dx(1) - dy(0))
        o_ref[7, r] = ent + 0.2 * -(vx * dx(6) + vy * dy(6) + vz * dz(6))


def on_device(state, shifts, fracs):
    variables, radii, height, width = state.shape
    count = variables * radii
    bands = lax.axis_size("rad")
    turned = lax.all_to_all(state.reshape(count, height, width), "az", 0, 0, tiled=True)
    moved = pl.pallas_call(
        remap_kernel,
        out_shape=jax.ShapeDtypeStruct((count, height + 8, width), F32),
        in_specs=[SMEM, SMEM, VMEM],
        out_specs=VMEM,
        compiler_params=GRANT,
        name="remap",
    )(shifts, fracs, turned)
    remapped = lax.all_to_all(moved, "az", 0, 0, tiled=True).reshape(
        variables, radii, height + 8, width
    )
    edge = jax.ShapeDtypeStruct((5, height, width), F32)
    chip, far = pl.pallas_call(
        edge_kernel, out_shape=(edge, edge), in_specs=[VMEM], out_specs=(VMEM, VMEM), name="edges",
        compiler_params=GRANT,
    )(remapped)
    inner = [(i, i ^ 1) for i in range(bands)]
    outer = [(i, i + 1) for i in range(1, bands - 1, 2)] + [(i + 1, i) for i in range(1, bands - 1, 2)]
    far = lax.ppermute(far, "rad", outer)
    chip = lax.ppermute(chip, "rad", inner)
    return pl.pallas_call(
        update_kernel,
        out_shape=jax.ShapeDtypeStruct(state.shape, F32),
        in_specs=[VMEM, VMEM, VMEM],
        out_specs=VMEM,
        scratch_shapes=[pltpu.VMEM((8, radii, height + 16, width), F32)],
        compiler_params=GRANT,
        name="update",
    )(remapped, chip, far)


def solution(mesh):
    in_specs = (P(None, "rad", None, "az"), P("rad"), P("rad"))
    out_specs = P(None, "rad", None, "az")
    return jax.shard_map(
        on_device, mesh=mesh, in_specs=in_specs, out_specs=out_specs, check_vma=False
    )
```

```python
import functools

import jax
import jax.numpy as jnp
from jax import lax
from jax.experimental import pallas as pl
from jax.experimental.pallas import tpu as pltpu
from jax.sharding import PartitionSpec as P

F32 = jnp.float32
VMEM = pl.BlockSpec(memory_space=pltpu.VMEM)
SMEM = pl.BlockSpec(memory_space=pltpu.SMEM)
ANY = pl.BlockSpec(memory_space=pl.ANY)
GRANT = pltpu.CompilerParams(vmem_limit_bytes=16 * 2**20)
ROWS = 8
EDGE_FIELDS = (1, 2, 3, 6, 7)
SIDE_FIELDS = (0, 2, 4, 6, 7)
EDGE_CHANGED = (0, 1, 5, 6, 7)
EDGE_SETTLED = (2, 3, 4)


def remap_kernel(shifts_ref, fracs_ref, x_ref, o_ref, ends_ref):
    blocks, height, width = x_ref.shape
    mine = lax.rem(lax.axis_index("az"), shifts_ref.shape[0])
    shift = shifts_ref[mine]
    frac = fracs_ref[mine]
    block_shift = lax.div(shift, width)
    lane_shift = lax.rem(shift, width)
    lane = lax.broadcasted_iota(jnp.int32, (height, width), 1)
    own = lane + lane_shift < width
    own_next = lane + lane_shift + 1 < width
    for i in range(blocks):
        near = x_ref[lax.rem(i - block_shift + blocks, blocks)]
        far = x_ref[lax.rem(i - block_shift - 1 + 2 * blocks, blocks)]
        first = pltpu.roll(jnp.where(own, near, far), lane_shift, 1)
        second = pltpu.roll(jnp.where(own_next, near, far), lane_shift + 1, 1)
        o_ref[i, :height, :] = (1.0 - frac) * first + frac * second
    slot = lax.broadcasted_iota(jnp.int32, (ROWS, width), 1)
    pair = lax.shift_right_logical(slot, 1)
    kept = [pair == k for k in range(height // ROWS)]
    for i in range(blocks):
        ends = jnp.zeros((ROWS, width), F32)
        for k in range(height // ROWS):
            turned = pltpu.roll(o_ref[i, k * ROWS : (k + 1) * ROWS, :], 2 * k + 1, 1)
            ends = jnp.where(kept[k], turned, ends)
        ends_ref[i] = ends
    odd = (slot & 1) == 1
    for i in range(blocks):
        before = pltpu.roll(ends_ref[(i - 1) % blocks], 1, 1)
        after = pltpu.roll(ends_ref[(i + 1) % blocks], width - 1, 1)
        o_ref[i, height:, :] = jnp.where(odd, before, after)


def products(S):
    rho, vx, vy, vz, bx, by, bz, ent = S
    return (
        vy * bz - vz * by,
        vz * bx - vx * bz,
        vx * by - vy * bx,
        rho * vx,
        rho * vy,
        rho * vz,
        ent,
        0.5 * (bx * bx + by * by + bz * bz),
    )


def edge_kernel(outward, s_ref, far_ref):
    height = far_ref.shape[1]
    odd = lax.rem(lax.axis_index("rad"), 2)
    r = (odd if outward else 1 - odd) * (s_ref.shape[1] - 1)
    fields = products([s_ref[v, r, :height] for v in range(8)])
    for at, field in enumerate(EDGE_FIELDS):
        far_ref[at] = fields[field]


def main_kernel(s_ref, o_ref, part_ref, f_ref, done_ref, sems):
    variables, radii, height, width = done_ref.shape
    bands = lax.axis_size("rad")
    band = lax.axis_index("rad")
    total_radii = radii * bands
    pad = ROWS
    lane = lax.broadcasted_iota(jnp.int32, (height, width), 1)
    level = lax.broadcasted_iota(jnp.int32, (height, width), 0)
    zk = (level.astype(F32) + 0.5) / height - 0.5
    for r in range(radii):
        for at, field in enumerate(products([s_ref[v, r, :height] for v in range(8)])):
            f_ref[at, r, pad : pad + height] = field
            f_ref[at, r, :pad] = jnp.zeros((pad, width), F32)
            f_ref[at, r, pad + height :] = jnp.zeros((pad, width), F32)
    copies = []
    for r in (1, 2, 0, 3):
        rho, vx, vy, vz, bx, by, bz, ent = [s_ref[v, r, :height] for v in range(8)]
        tails = products([s_ref[v, r, height:] for v in range(8)])
        xr = ((band * radii + r).astype(F32) + 0.5) / total_radii - 0.5
        outer = r == 0 or r == radii - 1

        def dx(at):
            if r == 0:
                return 0.5 * f_ref[at, 1, pad : pad + height]
            minus = f_ref[at, r - 1, pad : pad + height]
            if r == radii - 1:
                return -0.5 * minus
            return 0.5 * (f_ref[at, r + 1, pad : pad + height] - minus)

        def dy(at):
            here = f_ref[at, r, pad : pad + height]
            beside = jnp.concatenate(
                [pltpu.roll(tails[at], width - 2 * k - 1, 1) for k in range(height // ROWS)], axis=0
            )
            plus = jnp.where(lane == width - 1, beside, pltpu.roll(here, width - 1, 1))
            minus = jnp.where(lane == 0, beside, pltpu.roll(here, 1, 1))
            return 0.5 * (plus - minus)

        def dz(at):
            plus = f_ref[at, r, pad + 1 : pad + 1 + height]
            minus = f_ref[at, r, pad - 1 : pad - 1 + height]
            return 0.5 * (plus - minus)

        new = (
            rho + 0.2 * -(dx(3) + dy(4) + dz(5)),
            vx + 0.2 * (2.0 * vy + 3.0 * xr - dx(7)),
            vy + 0.2 * (-0.5 * vx - dy(7)),
            vz + 0.2 * (-zk - dz(7)),
            bx + 0.2 * (dy(2) - dz(1)),
            by + 0.2 * (dz(0) - dx(2)),
            bz + 0.2 * (dx(1) - dy(0)),
            ent + 0.2 * -(vx * dx(6) + vy * dy(6) + vz * dz(6)),
        )
        for v in range(variables):
            if outer and v in EDGE_CHANGED:
                part_ref[EDGE_CHANGED.index(v), r // (radii - 1)] = new[v]
            else:
                done_ref[v, r] = new[v]
        span = slice(EDGE_SETTLED[0], EDGE_SETTLED[-1] + 1) if outer else slice(0, variables)
        copy = pltpu.make_async_copy(done_ref.at[span, r], o_ref.at[span, r], sems.at[r])
        copy.start()
        copies.append(copy)
    for copy in copies:
        copy.wait()


def finish_kernel(base_ref, s_ref, part_ref, far_ref, chip_ref, o_ref, done_ref, sems):
    del base_ref
    radii = s_ref.shape[1]
    height = chip_ref.shape[1]
    odd = lax.rem(lax.axis_index("rad"), 2) == 1
    copies = []
    for pair in range(2):
        r = pair * (radii - 1)
        step = 0.1 if pair else -0.1
        halo = []
        for at in range(len(EDGE_FIELDS)):
            up, down = (far_ref, chip_ref) if pair else (chip_ref, far_ref)
            halo.append(step * jnp.where(odd, up[at], down[at]))
        wy, wz, fx, es, pm = halo
        vx = s_ref[1, r, :height]
        changes = (-fx, -pm, -wz, wy, -(vx * es))
        for at, v in enumerate(EDGE_CHANGED):
            done_ref[at, pair] = part_ref[at, pair] + changes[at]
            copy = pltpu.make_async_copy(done_ref.at[at, pair], o_ref.at[v, r], sems.at[at, pair])
            copy.start()
            copies.append(copy)
    for copy in copies:
        copy.wait()


def on_device(state, shifts, fracs):
    variables, radii, height, width = state.shape
    count = variables * radii
    bands = lax.axis_size("rad")
    turned = lax.all_to_all(state.reshape(count, height, width), "az", 0, 0, tiled=True)
    moved = pl.pallas_call(
        remap_kernel,
        out_shape=jax.ShapeDtypeStruct((count, height + ROWS, width), F32),
        in_specs=[SMEM, SMEM, VMEM],
        out_specs=VMEM,
        scratch_shapes=[pltpu.VMEM((count, ROWS, width), F32)],
        compiler_params=GRANT,
        name="remap",
    )(shifts, fracs, turned)
    remapped = lax.all_to_all(moved, "az", 0, 0, tiled=True).reshape(
        variables, radii, height + ROWS, width
    )
    edge = jax.ShapeDtypeStruct((len(EDGE_FIELDS), height, width), F32)
    far, chip = [
        pl.pallas_call(
            functools.partial(edge_kernel, outward),
            out_shape=edge,
            in_specs=[VMEM],
            out_specs=VMEM,
            compiler_params=GRANT,
            name="far_edge" if outward else "chip_edge",
        )(remapped)
        for outward in (True, False)
    ]
    odd = range(1, bands - 1, 2)
    far = lax.ppermute(far, "rad", [(i, i + 1) for i in odd] + [(i + 1, i) for i in odd])
    chip = lax.ppermute(chip, "rad", [(i, i ^ 1) for i in range(bands)])
    changed = len(EDGE_CHANGED)
    whole = jax.ShapeDtypeStruct(state.shape, F32)
    settled, part = pl.pallas_call(
        main_kernel,
        out_shape=(whole, jax.ShapeDtypeStruct((changed, 2, height, width), F32)),
        in_specs=[VMEM],
        out_specs=(ANY, VMEM),
        scratch_shapes=[
            pltpu.VMEM((8, radii, height + 2 * ROWS, width), F32),
            pltpu.VMEM(state.shape, F32),
            pltpu.SemaphoreType.DMA((radii,)),
        ],
        compiler_params=GRANT,
        cost_estimate=pl.CostEstimate(flops=4 * 10**6, bytes_accessed=4 * 2**20, transcendentals=0),
        name="main",
    )(remapped)
    return pl.pallas_call(
        finish_kernel,
        out_shape=whole,
        in_specs=[ANY, VMEM, VMEM, VMEM, VMEM],
        out_specs=ANY,
        scratch_shapes=[
            pltpu.VMEM((changed, 2, height, width), F32),
            pltpu.SemaphoreType.DMA((changed, 2)),
        ],
        input_output_aliases={0: 0},
        compiler_params=GRANT,
        name="finish",
    )(settled, remapped, part, far, chip)


def solution(mesh):
    in_specs = (P(None, "rad", None, "az"), P("rad"), P("rad"))
    out_specs = P(None, "rad", None, "az")
    return jax.shard_map(
        on_device, mesh=mesh, in_specs=in_specs, out_specs=out_specs, check_vma=False
    )
```

```python
import functools

import jax
import jax.numpy as jnp
from jax import lax
from jax.experimental import pallas as pl
from jax.experimental.pallas import tpu as pltpu
from jax.sharding import PartitionSpec as P

F32 = jnp.float32
VMEM = pl.BlockSpec(memory_space=pltpu.VMEM)
SMEM = pl.BlockSpec(memory_space=pltpu.SMEM)
ANY = pl.BlockSpec(memory_space=pl.ANY)
GRANT = pltpu.CompilerParams(vmem_limit_bytes=16 * 2**20)
ROWS = 8
EDGE_FIELDS = (1, 2, 3, 6, 7)
SIDE_FIELDS = (0, 2, 4, 6, 7)
EDGE_CHANGED = (0, 1, 5, 6, 7)
EDGE_SETTLED = (2, 3, 4)


def remap_kernel(shifts_ref, fracs_ref, x_ref, o_ref, ends_ref):
    blocks, height, width = x_ref.shape
    tall = height + 1
    mine = lax.rem(lax.axis_index("az"), shifts_ref.shape[0])
    shift = shifts_ref[mine]
    frac = fracs_ref[mine]
    block_shift = lax.div(shift, width)
    lane_shift = lax.rem(shift, width)
    lane = lax.broadcasted_iota(jnp.int32, (height, width), 1)
    own = lane + lane_shift < width
    own_next = lane + lane_shift + 1 < width
    for i in range(blocks):
        near = x_ref[lax.rem(i - block_shift + blocks, blocks)]
        far = x_ref[lax.rem(i - block_shift - 1 + 2 * blocks, blocks)]
        first = pltpu.roll(jnp.where(own, near, far), lane_shift, 1)
        second = pltpu.roll(jnp.where(own_next, near, far), lane_shift + 1, 1)
        o_ref[tall * i : tall * i + height, :] = (1.0 - frac) * first + frac * second
    pair = lax.shift_right_logical(lane, 1)
    ends = jnp.zeros((height, width), F32)
    for i in range(blocks):
        cells = o_ref[tall * i : tall * i + height, :]
        ends = jnp.where(pair == i, pltpu.roll(cells, (2 * i + 1) % width, 1), ends)
    rows = jnp.transpose(jnp.concatenate([ends, jnp.zeros((width - height, width), F32)], axis=0))
    used = 2 * blocks
    ends_ref[0] = rows[:used]
    ends_ref[1] = pltpu.roll(rows[:used], height, 1)
    for i in range(blocks):
        last = 2 * ((i - 1) % blocks)
        head = 2 * ((i + 1) % blocks) + 1
        at = tall * i + height
        o_ref[at : at + 1, :] = ends_ref[0, last : last + 1, :] + ends_ref[1, head : head + 1, :]


def slab(s_ref, at, height):
    return s_ref[at * (height + 1) : at * (height + 1) + height]


def products(S):
    rho, vx, vy, vz, bx, by, bz, ent = S
    return (
        vy * bz - vz * by,
        vz * bx - vx * bz,
        vx * by - vy * bx,
        rho * vx,
        rho * vy,
        rho * vz,
        ent,
        0.5 * (bx * bx + by * by + bz * bz),
    )


def edge_kernel(radii, s_ref, far_ref, chip_ref):
    height = far_ref.shape[1]
    odd = lax.rem(lax.axis_index("rad"), 2) == 1
    low = products([slab(s_ref, v * radii, height) for v in range(8)])
    high = products([slab(s_ref, v * radii + radii - 1, height) for v in range(8)])
    for at, field in enumerate(EDGE_FIELDS):
        far_ref[at] = jnp.where(odd, high[field], low[field])
        chip_ref[at] = jnp.where(odd, low[field], high[field])


def main_kernel(s_ref, o_ref, part_ref, f_ref, done_ref, sems):
    variables, radii, height, width = done_ref.shape
    bands = lax.axis_size("rad")
    band = lax.axis_index("rad")
    total_radii = radii * bands
    pad = ROWS
    tall = height + 1
    side = lax.broadcasted_iota(jnp.int32, (ROWS, width), 1)
    spot = lax.broadcasted_iota(jnp.int32, (ROWS, width), 0) + jnp.where(side == 0, 0, height)
    lane = lax.broadcasted_iota(jnp.int32, (height, width), 1)
    level = lax.broadcasted_iota(jnp.int32, (height, width), 0)
    zk = (level.astype(F32) + 0.5) / height - 0.5
    for r in range(radii):
        for at, field in enumerate(products([slab(s_ref, v * radii + r, height) for v in range(8)])):
            f_ref[at, r, pad : pad + height] = field
            f_ref[at, r, :pad] = jnp.zeros((pad, width), F32)
            f_ref[at, r, pad + height :] = jnp.zeros((pad, width), F32)
    copies = []
    for r in (1, 2, 0, 3):
        rho, vx, vy, vz, bx, by, bz, ent = [slab(s_ref, v * radii + r, height) for v in range(8)]
        tails = products([s_ref[(v * radii + r) * tall + height : (v * radii + r + 1) * tall] for v in range(8)])
        xr = ((band * radii + r).astype(F32) + 0.5) / total_radii - 0.5
        outer = r == 0 or r == radii - 1

        def dx(at):
            if r == 0:
                return 0.5 * f_ref[at, 1, pad : pad + height]
            minus = f_ref[at, r - 1, pad : pad + height]
            if r == radii - 1:
                return -0.5 * minus
            return 0.5 * (f_ref[at, r + 1, pad : pad + height] - minus)

        def dy(at):
            here = f_ref[at, r, pad : pad + height]
            row = jnp.broadcast_to(tails[at], (ROWS, width))
            next_to = jnp.concatenate(
                [
                    jnp.take_along_axis(row, spot + k * ROWS, axis=1, mode="promise_in_bounds")
                    for k in range(height // ROWS)
                ],
                axis=0,
            )
            plus = jnp.where(lane == width - 1, next_to, pltpu.roll(here, width - 1, 1))
            minus = jnp.where(lane == 0, next_to, pltpu.roll(here, 1, 1))
            return 0.5 * (plus - minus)

        def dz(at):
            plus = f_ref[at, r, pad + 1 : pad + 1 + height]
            minus = f_ref[at, r, pad - 1 : pad - 1 + height]
            return 0.5 * (plus - minus)

        new = (
            rho + 0.2 * -(dx(3) + dy(4) + dz(5)),
            vx + 0.2 * (2.0 * vy + 3.0 * xr - dx(7)),
            vy + 0.2 * (-0.5 * vx - dy(7)),
            vz + 0.2 * (-zk - dz(7)),
            bx + 0.2 * (dy(2) - dz(1)),
            by + 0.2 * (dz(0) - dx(2)),
            bz + 0.2 * (dx(1) - dy(0)),
            ent + 0.2 * -(vx * dx(6) + vy * dy(6) + vz * dz(6)),
        )
        for v in range(variables):
            if outer and v in EDGE_CHANGED:
                part_ref[EDGE_CHANGED.index(v), r // (radii - 1)] = new[v]
            else:
                done_ref[v, r] = new[v]
        span = slice(EDGE_SETTLED[0], EDGE_SETTLED[-1] + 1) if outer else slice(0, variables)
        copy = pltpu.make_async_copy(done_ref.at[span, r], o_ref.at[span, r], sems.at[r])
        copy.start()
        copies.append(copy)
    for copy in copies:
        copy.wait()


def finish_kernel(radii, base_ref, s_ref, part_ref, far_ref, chip_ref, o_ref, done_ref, sems):
    del base_ref
    height = chip_ref.shape[1]
    odd = lax.rem(lax.axis_index("rad"), 2) == 1
    copies = []
    for pair in range(2):
        r = pair * (radii - 1)
        step = 0.1 if pair else -0.1
        halo = []
        for at in range(len(EDGE_FIELDS)):
            up, down = (far_ref, chip_ref) if pair else (chip_ref, far_ref)
            halo.append(step * jnp.where(odd, up[at], down[at]))
        wy, wz, fx, es, pm = halo
        vx = slab(s_ref, radii + r, height)
        changes = (-fx, -pm, -wz, wy, -(vx * es))
        for at, v in enumerate(EDGE_CHANGED):
            done_ref[at, pair] = part_ref[at, pair] + changes[at]
            copy = pltpu.make_async_copy(done_ref.at[at, pair], o_ref.at[v, r], sems.at[at, pair])
            copy.start()
            copies.append(copy)
    for copy in copies:
        copy.wait()


def on_device(state, shifts, fracs):
    variables, radii, height, width = state.shape
    count = variables * radii
    bands = lax.axis_size("rad")
    turned = lax.all_to_all(state.reshape(count, height, width), "az", 0, 0, tiled=True)
    moved = pl.pallas_call(
        remap_kernel,
        out_shape=jax.ShapeDtypeStruct((count * (height + 1), width), F32),
        in_specs=[SMEM, SMEM, VMEM],
        out_specs=VMEM,
        scratch_shapes=[pltpu.VMEM((2, 2 * count, width), F32)],
        compiler_params=GRANT,
        name="remap",
    )(shifts, fracs, turned)
    moved = moved.reshape(count, height + 1, 1, width)
    remapped = lax.all_to_all(moved, "az", 0, 0, tiled=True).reshape(count * (height + 1), width)
    edge = jax.ShapeDtypeStruct((len(EDGE_FIELDS), height, width), F32)
    far, chip = pl.pallas_call(
        functools.partial(edge_kernel, radii),
        out_shape=(edge, edge),
        in_specs=[VMEM],
        out_specs=(VMEM, VMEM),
        compiler_params=GRANT,
        name="edges",
    )(remapped)
    odd = range(1, bands - 1, 2)
    far = lax.ppermute(far, "rad", [(i, i + 1) for i in odd] + [(i + 1, i) for i in odd])
    chip = lax.ppermute(chip, "rad", [(i, i ^ 1) for i in range(bands)])
    changed = len(EDGE_CHANGED)
    whole = jax.ShapeDtypeStruct(state.shape, F32)
    settled, part = pl.pallas_call(
        main_kernel,
        out_shape=(whole, jax.ShapeDtypeStruct((changed, 2, height, width), F32)),
        in_specs=[VMEM],
        out_specs=(ANY, VMEM),
        scratch_shapes=[
            pltpu.VMEM((8, radii, height + 2 * ROWS, width), F32),
            pltpu.VMEM(state.shape, F32),
            pltpu.SemaphoreType.DMA((radii,)),
        ],
        compiler_params=GRANT,
        cost_estimate=pl.CostEstimate(flops=4 * 10**6, bytes_accessed=4 * 2**20, transcendentals=0),
        name="main",
    )(remapped)
    return pl.pallas_call(
        functools.partial(finish_kernel, radii),
        out_shape=whole,
        in_specs=[ANY, VMEM, VMEM, VMEM, VMEM],
        out_specs=ANY,
        scratch_shapes=[
            pltpu.VMEM((changed, 2, height, width), F32),
            pltpu.SemaphoreType.DMA((changed, 2)),
        ],
        input_output_aliases={0: 0},
        compiler_params=GRANT,
        name="finish",
    )(settled, remapped, part, far, chip)


def solution(mesh):
    in_specs = (P(None, "rad", None, "az"), P("rad"), P("rad"))
    out_specs = P(None, "rad", None, "az")
    return jax.shard_map(
        on_device, mesh=mesh, in_specs=in_specs, out_specs=out_specs, check_vma=False
    )
```

```python
import functools

import jax
import jax.numpy as jnp
from jax import lax
from jax.experimental import pallas as pl
from jax.experimental.pallas import tpu as pltpu
from jax.sharding import PartitionSpec as P

F32 = jnp.float32
VMEM = pl.BlockSpec(memory_space=pltpu.VMEM)
SMEM = pl.BlockSpec(memory_space=pltpu.SMEM)
ANY = pl.BlockSpec(memory_space=pl.ANY)
GRANT = pltpu.CompilerParams(vmem_limit_bytes=16 * 2**20)
ROWS = 8
EDGE_FIELDS = (1, 2, 3, 6, 7)
SIDE_FIELDS = (0, 2, 4, 6, 7)
EDGE_CHANGED = (0, 1, 5, 6, 7)
EDGE_SETTLED = (2, 3, 4)


def remap_kernel(shifts_ref, fracs_ref, x_ref, o_ref, ends_ref):
    blocks, height, width = x_ref.shape
    tall = height + 1
    mine = lax.rem(lax.axis_index("az"), shifts_ref.shape[0])
    shift = shifts_ref[mine]
    frac = fracs_ref[mine]
    block_shift = lax.div(shift, width)
    lane_shift = lax.rem(shift, width)
    lane = lax.broadcasted_iota(jnp.int32, (height, width), 1)
    own = lane + lane_shift < width
    own_next = lane + lane_shift + 1 < width
    for i in range(blocks):
        near = x_ref[lax.rem(i - block_shift + blocks, blocks)]
        far = x_ref[lax.rem(i - block_shift - 1 + 2 * blocks, blocks)]
        first = pltpu.roll(jnp.where(own, near, far), lane_shift, 1)
        second = pltpu.roll(jnp.where(own_next, near, far), lane_shift + 1, 1)
        o_ref[tall * i : tall * i + height, :] = (1.0 - frac) * first + frac * second
    pair = lax.shift_right_logical(lane, 1)
    ends = jnp.zeros((height, width), F32)
    for i in range(blocks):
        cells = o_ref[tall * i : tall * i + height, :]
        ends = jnp.where(pair == i, pltpu.roll(cells, (2 * i + 1) % width, 1), ends)
    rows = jnp.transpose(jnp.concatenate([ends, jnp.zeros((width - height, width), F32)], axis=0))
    used = 2 * blocks
    ends_ref[0] = rows[:used]
    ends_ref[1] = pltpu.roll(rows[:used], height, 1)
    for i in range(blocks):
        last = 2 * ((i - 1) % blocks)
        head = 2 * ((i + 1) % blocks) + 1
        at = tall * i + height
        o_ref[at : at + 1, :] = ends_ref[0, last : last + 1, :] + ends_ref[1, head : head + 1, :]


def slab(s_ref, at, height):
    return s_ref[at * (height + 1) : at * (height + 1) + height]


def products(S):
    rho, vx, vy, vz, bx, by, bz, ent = S
    return (
        vy * bz - vz * by,
        vz * bx - vx * bz,
        vx * by - vy * bx,
        rho * vx,
        rho * vy,
        rho * vz,
        ent,
        0.5 * (bx * bx + by * by + bz * bz),
    )


def edge_kernel(radii, s_ref, far_ref, chip_ref):
    height = far_ref.shape[1]
    odd = lax.rem(lax.axis_index("rad"), 2) == 1
    low = products([slab(s_ref, v * radii, height) for v in range(8)])
    high = products([slab(s_ref, v * radii + radii - 1, height) for v in range(8)])
    for at, field in enumerate(EDGE_FIELDS):
        far_ref[at] = jnp.where(odd, high[field], low[field])
        chip_ref[at] = jnp.where(odd, low[field], high[field])


def main_kernel(s_ref, o_ref, part_ref, f_ref, done_ref, sems):
    variables, radii, height, width = done_ref.shape
    bands = lax.axis_size("rad")
    band = lax.axis_index("rad")
    total_radii = radii * bands
    pad = ROWS
    tall = height + 1
    side = lax.broadcasted_iota(jnp.int32, (ROWS, width), 1)
    spot = lax.broadcasted_iota(jnp.int32, (ROWS, width), 0) + jnp.where(side == 0, 0, height)
    lane = lax.broadcasted_iota(jnp.int32, (height, width), 1)
    level = lax.broadcasted_iota(jnp.int32, (height, width), 0)
    zk = (level.astype(F32) + 0.5) / height - 0.5
    for r in range(radii):
        for at, field in enumerate(products([slab(s_ref, v * radii + r, height) for v in range(8)])):
            f_ref[at, r, pad : pad + height] = field
            f_ref[at, r, :pad] = jnp.zeros((pad, width), F32)
            f_ref[at, r, pad + height :] = jnp.zeros((pad, width), F32)
    copies = []
    for r in (1, 2, 0, 3):
        rho, vx, vy, vz, bx, by, bz, ent = [slab(s_ref, v * radii + r, height) for v in range(8)]
        tails = products([s_ref[(v * radii + r) * tall + height : (v * radii + r + 1) * tall] for v in range(8)])
        xr = ((band * radii + r).astype(F32) + 0.5) / total_radii - 0.5
        outer = r == 0 or r == radii - 1

        def dx(at):
            if r == 0:
                return 0.5 * f_ref[at, 1, pad : pad + height]
            minus = f_ref[at, r - 1, pad : pad + height]
            if r == radii - 1:
                return -0.5 * minus
            return 0.5 * (f_ref[at, r + 1, pad : pad + height] - minus)

        def dy(at):
            here = f_ref[at, r, pad : pad + height]
            row = jnp.broadcast_to(tails[at], (ROWS, width))
            next_to = jnp.concatenate(
                [
                    jnp.take_along_axis(row, spot + k * ROWS, axis=1, mode="promise_in_bounds")
                    for k in range(height // ROWS)
                ],
                axis=0,
            )
            plus = jnp.where(lane == width - 1, next_to, pltpu.roll(here, width - 1, 1))
            minus = jnp.where(lane == 0, next_to, pltpu.roll(here, 1, 1))
            return 0.5 * (plus - minus)

        def dz(at):
            plus = f_ref[at, r, pad + 1 : pad + 1 + height]
            minus = f_ref[at, r, pad - 1 : pad - 1 + height]
            return 0.5 * (plus - minus)

        new = (
            rho + 0.2 * -(dx(3) + dy(4) + dz(5)),
            vx + 0.2 * (2.0 * vy + 3.0 * xr - dx(7)),
            vy + 0.2 * (-0.5 * vx - dy(7)),
            vz + 0.2 * (-zk - dz(7)),
            bx + 0.2 * (dy(2) - dz(1)),
            by + 0.2 * (dz(0) - dx(2)),
            bz + 0.2 * (dx(1) - dy(0)),
            ent + 0.2 * -(vx * dx(6) + vy * dy(6) + vz * dz(6)),
        )
        for v in range(variables):
            if outer and v in EDGE_CHANGED:
                part_ref[EDGE_CHANGED.index(v), r // (radii - 1)] = new[v]
            else:
                done_ref[v, r] = new[v]
        span = slice(EDGE_SETTLED[0], EDGE_SETTLED[-1] + 1) if outer else slice(0, variables)
        copy = pltpu.make_async_copy(done_ref.at[span, r], o_ref.at[span, r], sems.at[r])
        copy.start()
        copies.append(copy)
    for copy in copies:
        copy.wait()


def relay_kernel(from_ref, part_ref, to_ref):
    del part_ref
    to_ref[...] = from_ref[...]


def finish_kernel(radii, base_ref, s_ref, part_ref, below_ref, chip_ref, above_ref, o_ref, done_ref, sems):
    del base_ref
    height = chip_ref.shape[1]
    odd = lax.rem(lax.axis_index("rad"), 2) == 1
    copies = []
    for pair in range(2):
        r = pair * (radii - 1)
        step = 0.1 if pair else -0.1
        halo = []
        for at in range(len(EDGE_FIELDS)):
            outside = above_ref[at] if pair else below_ref[at]
            far_here = odd if pair else jnp.logical_not(odd)
            halo.append(step * jnp.where(far_here, outside, chip_ref[at]))
        wy, wz, fx, es, pm = halo
        vx = slab(s_ref, radii + r, height)
        changes = (-fx, -pm, -wz, wy, -(vx * es))
        for at, v in enumerate(EDGE_CHANGED):
            done_ref[at, pair] = part_ref[at, pair] + changes[at]
            copy = pltpu.make_async_copy(done_ref.at[at, pair], o_ref.at[v, r], sems.at[at, pair])
            copy.start()
            copies.append(copy)
    for copy in copies:
        copy.wait()


def on_device(state, shifts, fracs):
    variables, radii, height, width = state.shape
    count = variables * radii
    bands = lax.axis_size("rad")
    turned = lax.all_to_all(state.reshape(count, height, width), "az", 0, 0, tiled=True)
    moved = pl.pallas_call(
        remap_kernel,
        out_shape=jax.ShapeDtypeStruct((count * (height + 1), width), F32),
        in_specs=[SMEM, SMEM, VMEM],
        out_specs=VMEM,
        scratch_shapes=[pltpu.VMEM((2, 2 * count, width), F32)],
        compiler_params=GRANT,
        name="remap",
    )(shifts, fracs, turned)
    moved = moved.reshape(count, height + 1, 1, width)
    remapped = lax.all_to_all(moved, "az", 0, 0, tiled=True).reshape(count * (height + 1), width)
    edge = jax.ShapeDtypeStruct((len(EDGE_FIELDS), height, width), F32)
    far, chip = pl.pallas_call(
        functools.partial(edge_kernel, radii),
        out_shape=(edge, edge),
        in_specs=[VMEM],
        out_specs=(VMEM, VMEM),
        compiler_params=GRANT,
        name="edges",
    )(remapped)
    odd = range(1, bands - 1, 2)
    relayed = lax.ppermute(far, "rad", [(i, i + 2) for i in odd])
    above = lax.ppermute(far, "rad", [(i + 1, i) for i in odd])
    chip = lax.ppermute(chip, "rad", [(i, i ^ 1) for i in range(bands)])
    changed = len(EDGE_CHANGED)
    whole = jax.ShapeDtypeStruct(state.shape, F32)
    settled, part = pl.pallas_call(
        main_kernel,
        out_shape=(whole, jax.ShapeDtypeStruct((changed, 2, height, width), F32)),
        in_specs=[VMEM],
        out_specs=(ANY, VMEM),
        scratch_shapes=[
            pltpu.VMEM((8, radii, height + 2 * ROWS, width), F32),
            pltpu.VMEM(state.shape, F32),
            pltpu.SemaphoreType.DMA((radii,)),
        ],
        compiler_params=GRANT,
        cost_estimate=pl.CostEstimate(flops=4000000000, bytes_accessed=4 * 2**20, transcendentals=0),
        name="main",
    )(remapped)
    relayed = pl.pallas_call(
        relay_kernel,
        out_shape=edge,
        in_specs=[VMEM, ANY],
        out_specs=VMEM,
        compiler_params=GRANT,
        name="relay",
    )(relayed, part)
    below = lax.ppermute(relayed, "rad", [(i + 2, i + 1) for i in odd])
    return pl.pallas_call(
        functools.partial(finish_kernel, radii),
        out_shape=whole,
        in_specs=[ANY, VMEM, VMEM, VMEM, VMEM, VMEM],
        out_specs=ANY,
        scratch_shapes=[
            pltpu.VMEM((changed, 2, height, width), F32),
            pltpu.SemaphoreType.DMA((changed, 2)),
        ],
        input_output_aliases={0: 0},
        compiler_params=GRANT,
        name="finish",
    )(settled, remapped, part, below, chip, above)


def solution(mesh):
    in_specs = (P(None, "rad", None, "az"), P("rad"), P("rad"))
    out_specs = P(None, "rad", None, "az")
    return jax.shard_map(
        on_device, mesh=mesh, in_specs=in_specs, out_specs=out_specs, check_vma=False
    )
```

```python
import functools

import jax
import jax.numpy as jnp
from jax import lax
from jax.experimental import pallas as pl
from jax.experimental.pallas import tpu as pltpu
from jax.sharding import PartitionSpec as P

F32 = jnp.float32
VMEM = pl.BlockSpec(memory_space=pltpu.VMEM)
SMEM = pl.BlockSpec(memory_space=pltpu.SMEM)
ANY = pl.BlockSpec(memory_space=pl.ANY)
GRANT = pltpu.CompilerParams(vmem_limit_bytes=16 * 2**20)
ROWS = 8
EDGE_FIELDS = (1, 2, 3, 6, 7)
SIDE_FIELDS = (0, 2, 4, 6, 7)
EDGE_CHANGED = (0, 1, 5, 6, 7)
EDGE_SETTLED = (2, 3, 4)


def remap_kernel(shifts_ref, fracs_ref, x_ref, o_ref, ends_ref):
    blocks, height, width = x_ref.shape
    tall = height + 1
    mine = lax.rem(lax.axis_index("az"), shifts_ref.shape[0])
    shift = shifts_ref[mine]
    frac = fracs_ref[mine]
    block_shift = lax.div(shift, width)
    lane_shift = lax.rem(shift, width)
    lane = lax.broadcasted_iota(jnp.int32, (height, width), 1)
    own = lane + lane_shift < width
    own_next = lane + lane_shift + 1 < width
    for i in range(blocks):
        near = x_ref[lax.rem(i - block_shift + blocks, blocks)]
        far = x_ref[lax.rem(i - block_shift - 1 + 2 * blocks, blocks)]
        first = pltpu.roll(jnp.where(own, near, far), lane_shift, 1)
        second = pltpu.roll(jnp.where(own_next, near, far), lane_shift + 1, 1)
        o_ref[tall * i : tall * i + height, :] = (1.0 - frac) * first + frac * second
    pair = lax.shift_right_logical(lane, 1)
    ends = jnp.zeros((height, width), F32)
    for i in range(blocks):
        cells = o_ref[tall * i : tall * i + height, :]
        ends = jnp.where(pair == i, pltpu.roll(cells, (2 * i + 1) % width, 1), ends)
    rows = jnp.transpose(jnp.concatenate([ends, jnp.zeros((width - height, width), F32)], axis=0))
    used = 2 * blocks
    ends_ref[0] = rows[:used]
    ends_ref[1] = pltpu.roll(rows[:used], height, 1)
    for i in range(blocks):
        last = 2 * ((i - 1) % blocks)
        head = 2 * ((i + 1) % blocks) + 1
        at = tall * i + height
        o_ref[at : at + 1, :] = ends_ref[0, last : last + 1, :] + ends_ref[1, head : head + 1, :]


def slab(s_ref, at, height):
    return s_ref[at * (height + 1) : at * (height + 1) + height]


def products(S):
    rho, vx, vy, vz, bx, by, bz, ent = S
    return (
        vy * bz - vz * by,
        vz * bx - vx * bz,
        vx * by - vy * bx,
        rho * vx,
        rho * vy,
        rho * vz,
        ent,
        0.5 * (bx * bx + by * by + bz * bz),
    )


def edge_kernel(radii, s_ref, far_ref, chip_ref):
    height = far_ref.shape[1]
    odd = lax.rem(lax.axis_index("rad"), 2) == 1
    low = products([slab(s_ref, v * radii, height) for v in range(8)])
    high = products([slab(s_ref, v * radii + radii - 1, height) for v in range(8)])
    for at, field in enumerate(EDGE_FIELDS):
        far_ref[at] = jnp.where(odd, high[field], low[field])
        chip_ref[at] = jnp.where(odd, low[field], high[field])


def main_kernel(s_ref, o_ref, part_ref, f_ref, done_ref, sems):
    variables, radii, height, width = done_ref.shape
    bands = lax.axis_size("rad")
    band = lax.axis_index("rad")
    total_radii = radii * bands
    pad = ROWS
    tall = height + 1
    side = lax.broadcasted_iota(jnp.int32, (ROWS, width), 1)
    spot = lax.broadcasted_iota(jnp.int32, (ROWS, width), 0) + jnp.where(side == 0, 0, height)
    lane = lax.broadcasted_iota(jnp.int32, (height, width), 1)
    level = lax.broadcasted_iota(jnp.int32, (height, width), 0)
    zk = (level.astype(F32) + 0.5) / height - 0.5
    for r in range(radii):
        for at, field in enumerate(products([slab(s_ref, v * radii + r, height) for v in range(8)])):
            f_ref[at, r, pad : pad + height] = field
            f_ref[at, r, :pad] = jnp.zeros((pad, width), F32)
            f_ref[at, r, pad + height :] = jnp.zeros((pad, width), F32)
    copies = []
    for r in (1, 2, 0, 3):
        rho, vx, vy, vz, bx, by, bz, ent = [slab(s_ref, v * radii + r, height) for v in range(8)]
        tails = products([s_ref[(v * radii + r) * tall + height : (v * radii + r + 1) * tall] for v in range(8)])
        xr = ((band * radii + r).astype(F32) + 0.5) / total_radii - 0.5
        outer = r == 0 or r == radii - 1

        def dx(at):
            if r == 0:
                return 0.5 * f_ref[at, 1, pad : pad + height]
            minus = f_ref[at, r - 1, pad : pad + height]
            if r == radii - 1:
                return -0.5 * minus
            return 0.5 * (f_ref[at, r + 1, pad : pad + height] - minus)

        def dy(at):
            here = f_ref[at, r, pad : pad + height]
            row = jnp.broadcast_to(tails[at], (ROWS, width))
            next_to = jnp.concatenate(
                [
                    jnp.take_along_axis(row, spot + k * ROWS, axis=1, mode="promise_in_bounds")
                    for k in range(height // ROWS)
                ],
                axis=0,
            )
            plus = jnp.where(lane == width - 1, next_to, pltpu.roll(here, width - 1, 1))
            minus = jnp.where(lane == 0, next_to, pltpu.roll(here, 1, 1))
            return 0.5 * (plus - minus)

        def dz(at):
            plus = f_ref[at, r, pad + 1 : pad + 1 + height]
            minus = f_ref[at, r, pad - 1 : pad - 1 + height]
            return 0.5 * (plus - minus)

        new = (
            rho + 0.2 * -(dx(3) + dy(4) + dz(5)),
            vx + 0.2 * (2.0 * vy + 3.0 * xr - dx(7)),
            vy + 0.2 * (-0.5 * vx - dy(7)),
            vz + 0.2 * (-zk - dz(7)),
            bx + 0.2 * (dy(2) - dz(1)),
            by + 0.2 * (dz(0) - dx(2)),
            bz + 0.2 * (dx(1) - dy(0)),
            ent + 0.2 * -(vx * dx(6) + vy * dy(6) + vz * dz(6)),
        )
        for v in range(variables):
            if outer and v in EDGE_CHANGED:
                part_ref[EDGE_CHANGED.index(v), r // (radii - 1)] = new[v]
            else:
                done_ref[v, r] = new[v]
        span = slice(EDGE_SETTLED[0], EDGE_SETTLED[-1] + 1) if outer else slice(0, variables)
        copy = pltpu.make_async_copy(done_ref.at[span, r], o_ref.at[span, r], sems.at[r])
        copy.start()
        copies.append(copy)
    for copy in copies:
        copy.wait()


def relay_kernel(from_ref, part_ref, to_ref):
    del part_ref
    to_ref[...] = from_ref[...]


def finish_kernel(radii, base_ref, s_ref, part_ref, below_ref, chip_ref, above_ref, o_ref, done_ref, sems):
    del base_ref
    height = chip_ref.shape[1]
    odd = lax.rem(lax.axis_index("rad"), 2) == 1
    copies = []
    for pair in range(2):
        r = pair * (radii - 1)
        step = 0.1 if pair else -0.1
        halo = []
        for at in range(len(EDGE_FIELDS)):
            outside = above_ref[at] if pair else below_ref[at]
            far_here = odd if pair else jnp.logical_not(odd)
            halo.append(step * jnp.where(far_here, outside, chip_ref[at]))
        wy, wz, fx, es, pm = halo
        vx = slab(s_ref, radii + r, height)
        changes = (-fx, -pm, -wz, wy, -(vx * es))
        for group, (begin, end) in enumerate(((0, 2), (2, 5))):
            for at in range(begin, end):
                done_ref[pair, at] = part_ref[at, pair] + changes[at]
            first = EDGE_CHANGED[begin]
            copy = pltpu.make_async_copy(
                done_ref.at[pair, begin:end],
                o_ref.at[first : first + end - begin, r],
                sems.at[group, pair],
            )
            copy.start()
            copies.append(copy)
    for copy in copies:
        copy.wait()


def on_device(state, shifts, fracs):
    variables, radii, height, width = state.shape
    count = variables * radii
    bands = lax.axis_size("rad")
    turned = lax.all_to_all(state.reshape(count, height, width), "az", 0, 0, tiled=True)
    moved = pl.pallas_call(
        remap_kernel,
        out_shape=jax.ShapeDtypeStruct((count * (height + 1), width), F32),
        in_specs=[SMEM, SMEM, VMEM],
        out_specs=VMEM,
        scratch_shapes=[pltpu.VMEM((2, 2 * count, width), F32)],
        compiler_params=GRANT,
        name="remap",
    )(shifts, fracs, turned)
    moved = moved.reshape(count, height + 1, 1, width)
    remapped = lax.all_to_all(moved, "az", 0, 0, tiled=True).reshape(count * (height + 1), width)
    edge = jax.ShapeDtypeStruct((len(EDGE_FIELDS), height, width), F32)
    far, chip = pl.pallas_call(
        functools.partial(edge_kernel, radii),
        out_shape=(edge, edge),
        in_specs=[VMEM],
        out_specs=(VMEM, VMEM),
        compiler_params=GRANT,
        name="edges",
    )(remapped)
    odd = range(1, bands - 1, 2)
    relayed = lax.ppermute(far, "rad", [(i, i + 2) for i in odd])
    above = lax.ppermute(far, "rad", [(i + 1, i) for i in odd])
    chip = lax.ppermute(chip, "rad", [(i, i ^ 1) for i in range(bands)])
    changed = len(EDGE_CHANGED)
    whole = jax.ShapeDtypeStruct(state.shape, F32)
    settled, part = pl.pallas_call(
        main_kernel,
        out_shape=(whole, jax.ShapeDtypeStruct((changed, 2, height, width), F32)),
        in_specs=[VMEM],
        out_specs=(ANY, VMEM),
        scratch_shapes=[
            pltpu.VMEM((8, radii, height + 2 * ROWS, width), F32),
            pltpu.VMEM(state.shape, F32),
            pltpu.SemaphoreType.DMA((radii,)),
        ],
        compiler_params=GRANT,
        cost_estimate=pl.CostEstimate(flops=4000000000, bytes_accessed=4 * 2**20, transcendentals=0),
        name="main",
    )(remapped)
    relayed = pl.pallas_call(
        relay_kernel,
        out_shape=edge,
        in_specs=[VMEM, ANY],
        out_specs=VMEM,
        compiler_params=GRANT,
        name="relay",
    )(relayed, part)
    below = lax.ppermute(relayed, "rad", [(i + 2, i + 1) for i in odd])
    return pl.pallas_call(
        functools.partial(finish_kernel, radii),
        out_shape=whole,
        in_specs=[ANY, VMEM, VMEM, VMEM, VMEM, VMEM],
        out_specs=ANY,
        scratch_shapes=[
            pltpu.VMEM((2, changed, height, width), F32),
            pltpu.SemaphoreType.DMA((2, 2)),
        ],
        input_output_aliases={0: 0},
        compiler_params=GRANT,
        name="finish",
    )(settled, remapped, part, below, chip, above)


def solution(mesh):
    in_specs = (P(None, "rad", None, "az"), P("rad"), P("rad"))
    out_specs = P(None, "rad", None, "az")
    return jax.shard_map(
        on_device, mesh=mesh, in_specs=in_specs, out_specs=out_specs, check_vma=False
    )
```

```python
import functools

import jax
import jax.numpy as jnp
from jax import lax
from jax.experimental import pallas as pl
from jax.experimental.pallas import tpu as pltpu
from jax.sharding import PartitionSpec as P

F32 = jnp.float32
VMEM = pl.BlockSpec(memory_space=pltpu.VMEM)
SMEM = pl.BlockSpec(memory_space=pltpu.SMEM)
ANY = pl.BlockSpec(memory_space=pl.ANY)
GRANT = pltpu.CompilerParams(vmem_limit_bytes=16 * 2**20)
ROWS = 8
EDGE_FIELDS = (1, 2, 3, 6, 7)
SIDE_FIELDS = (0, 2, 4, 6, 7)
EDGE_CHANGED = (0, 1, 5, 6, 7)
EDGE_SETTLED = (2, 3, 4)


def remap_kernel(shifts_ref, fracs_ref, x_ref, o_ref, ends_ref):
    blocks, height, width = x_ref.shape
    tall = height + 1
    mine = lax.rem(lax.axis_index("az"), shifts_ref.shape[0])
    shift = shifts_ref[mine]
    frac = fracs_ref[mine]
    block_shift = lax.div(shift, width)
    lane_shift = lax.rem(shift, width)
    next_shift = lax.rem(lane_shift + 1, width)
    lane = lax.broadcasted_iota(jnp.int32, (height, width), 1)
    own = lane + lane_shift < width
    own_next = lane + lane_shift + 1 < width
    for i in range(blocks):
        near = x_ref[lax.rem(i - block_shift + blocks, blocks)]
        far = x_ref[lax.rem(i - block_shift - 1 + 2 * blocks, blocks)]
        first = pltpu.roll(jnp.where(own, near, far), lane_shift, 1)
        second = pltpu.roll(jnp.where(own_next, near, far), next_shift, 1)
        o_ref[tall * i : tall * i + height, :] = (1.0 - frac) * first + frac * second
    pair = lax.shift_right_logical(lane, 1)
    ends = jnp.zeros((height, width), F32)
    for i in range(blocks):
        cells = o_ref[tall * i : tall * i + height, :]
        ends = jnp.where(pair == i, pltpu.roll(cells, (2 * i + 1) % width, 1), ends)
    rows = jnp.transpose(jnp.concatenate([ends, jnp.zeros((width - height, width), F32)], axis=0))
    used = 2 * blocks
    ends_ref[0] = rows[:used]
    ends_ref[1] = pltpu.roll(rows[:used], height, 1)
    for i in range(blocks):
        last = 2 * ((i - 1) % blocks)
        head = 2 * ((i + 1) % blocks) + 1
        at = tall * i + height
        o_ref[at : at + 1, :] = ends_ref[0, last : last + 1, :] + ends_ref[1, head : head + 1, :]


def slab(s_ref, at, height):
    return s_ref[at * (height + 1) : at * (height + 1) + height]


def products(S):
    rho, vx, vy, vz, bx, by, bz, ent = S
    return (
        vy * bz - vz * by,
        vz * bx - vx * bz,
        vx * by - vy * bx,
        rho * vx,
        rho * vy,
        rho * vz,
        ent,
        0.5 * (bx * bx + by * by + bz * bz),
    )


def edge_kernel(radii, s_ref, far_ref, chip_ref):
    height = far_ref.shape[1]
    odd = lax.rem(lax.axis_index("rad"), 2) == 1
    low = products([slab(s_ref, v * radii, height) for v in range(8)])
    high = products([slab(s_ref, v * radii + radii - 1, height) for v in range(8)])
    for at, field in enumerate(EDGE_FIELDS):
        far_ref[at] = jnp.where(odd, high[field], low[field])
        chip_ref[at] = jnp.where(odd, low[field], high[field])


def main_kernel(s_ref, o_ref, part_ref, f_ref, done_ref, sems):
    variables, radii, height, width = done_ref.shape
    bands = lax.axis_size("rad")
    band = lax.axis_index("rad")
    total_radii = radii * bands
    pad = ROWS
    tall = height + 1
    side = lax.broadcasted_iota(jnp.int32, (ROWS, width), 1)
    spot = lax.broadcasted_iota(jnp.int32, (ROWS, width), 0) + jnp.where(side == 0, 0, height)
    lane = lax.broadcasted_iota(jnp.int32, (height, width), 1)
    level = lax.broadcasted_iota(jnp.int32, (height, width), 0)
    zk = (level.astype(F32) + 0.5) / height - 0.5
    for r in range(radii):
        for at, field in enumerate(products([slab(s_ref, v * radii + r, height) for v in range(8)])):
            f_ref[at, r, pad : pad + height] = field
            f_ref[at, r, :pad] = jnp.zeros((pad, width), F32)
            f_ref[at, r, pad + height :] = jnp.zeros((pad, width), F32)
    copies = []
    for r in (1, 2, 0, 3):
        rho, vx, vy, vz, bx, by, bz, ent = [slab(s_ref, v * radii + r, height) for v in range(8)]
        tails = products([s_ref[(v * radii + r) * tall + height : (v * radii + r + 1) * tall] for v in range(8)])
        xr = ((band * radii + r).astype(F32) + 0.5) / total_radii - 0.5
        outer = r == 0 or r == radii - 1

        def dx(at):
            if r == 0:
                return 0.5 * f_ref[at, 1, pad : pad + height]
            minus = f_ref[at, r - 1, pad : pad + height]
            if r == radii - 1:
                return -0.5 * minus
            return 0.5 * (f_ref[at, r + 1, pad : pad + height] - minus)

        def dy(at):
            here = f_ref[at, r, pad : pad + height]
            row = jnp.broadcast_to(tails[at], (ROWS, width))
            next_to = jnp.concatenate(
                [
                    jnp.take_along_axis(row, spot + k * ROWS, axis=1, mode="promise_in_bounds")
                    for k in range(height // ROWS)
                ],
                axis=0,
            )
            plus = jnp.where(lane == width - 1, next_to, pltpu.roll(here, width - 1, 1))
            minus = jnp.where(lane == 0, next_to, pltpu.roll(here, 1, 1))
            return 0.5 * (plus - minus)

        def dz(at):
            plus = f_ref[at, r, pad + 1 : pad + 1 + height]
            minus = f_ref[at, r, pad - 1 : pad - 1 + height]
            return 0.5 * (plus - minus)

        new = (
            rho + 0.2 * -(dx(3) + dy(4) + dz(5)),
            vx + 0.2 * (2.0 * vy + 3.0 * xr - dx(7)),
            vy + 0.2 * (-0.5 * vx - dy(7)),
            vz + 0.2 * (-zk - dz(7)),
            bx + 0.2 * (dy(2) - dz(1)),
            by + 0.2 * (dz(0) - dx(2)),
            bz + 0.2 * (dx(1) - dy(0)),
            ent + 0.2 * -(vx * dx(6) + vy * dy(6) + vz * dz(6)),
        )
        for v in range(variables):
            if outer and v in EDGE_CHANGED:
                part_ref[EDGE_CHANGED.index(v), r // (radii - 1)] = new[v]
            else:
                done_ref[v, r] = new[v]
        span = slice(EDGE_SETTLED[0], EDGE_SETTLED[-1] + 1) if outer else slice(0, variables)
        copy = pltpu.make_async_copy(done_ref.at[span, r], o_ref.at[span, r], sems.at[r])
        copy.start()
        copies.append(copy)
    for copy in copies:
        copy.wait()


def relay_kernel(from_ref, part_ref, to_ref):
    del part_ref
    to_ref[...] = from_ref[...]


def finish_kernel(radii, base_ref, s_ref, part_ref, below_ref, chip_ref, above_ref, o_ref, done_ref, sems):
    del base_ref
    height = chip_ref.shape[1]
    odd = lax.rem(lax.axis_index("rad"), 2) == 1
    copies = []
    for pair in range(2):
        r = pair * (radii - 1)
        step = 0.1 if pair else -0.1
        halo = []
        for at in range(len(EDGE_FIELDS)):
            outside = above_ref[at] if pair else below_ref[at]
            far_here = odd if pair else jnp.logical_not(odd)
            halo.append(step * jnp.where(far_here, outside, chip_ref[at]))
        wy, wz, fx, es, pm = halo
        vx = slab(s_ref, radii + r, height)
        changes = (-fx, -pm, -wz, wy, -(vx * es))
        for group, (begin, end) in enumerate(((0, 2), (2, 5))):
            for at in range(begin, end):
                done_ref[pair, at] = part_ref[at, pair] + changes[at]
            first = EDGE_CHANGED[begin]
            copy = pltpu.make_async_copy(
                done_ref.at[pair, begin:end],
                o_ref.at[first : first + end - begin, r],
                sems.at[group, pair],
            )
            copy.start()
            copies.append(copy)
    for copy in copies:
        copy.wait()


def on_device(state, shifts, fracs):
    variables, radii, height, width = state.shape
    count = variables * radii
    bands = lax.axis_size("rad")
    turned = lax.all_to_all(state.reshape(count, height, width), "az", 0, 0, tiled=True)
    moved = pl.pallas_call(
        remap_kernel,
        out_shape=jax.ShapeDtypeStruct((count * (height + 1), width), F32),
        in_specs=[SMEM, SMEM, VMEM],
        out_specs=VMEM,
        scratch_shapes=[pltpu.VMEM((2, 2 * count, width), F32)],
        compiler_params=GRANT,
        name="remap",
    )(shifts, fracs, turned)
    moved = moved.reshape(count, height + 1, 1, width)
    remapped = lax.all_to_all(moved, "az", 0, 0, tiled=True).reshape(count * (height + 1), width)
    edge = jax.ShapeDtypeStruct((len(EDGE_FIELDS), height, width), F32)
    far, chip = pl.pallas_call(
        functools.partial(edge_kernel, radii),
        out_shape=(edge, edge),
        in_specs=[VMEM],
        out_specs=(VMEM, VMEM),
        compiler_params=GRANT,
        name="edges",
    )(remapped)
    odd = range(1, bands - 1, 2)
    relayed = lax.ppermute(far, "rad", [(i, i + 2) for i in odd])
    above = lax.ppermute(far, "rad", [(i + 1, i) for i in odd])
    chip = lax.ppermute(chip, "rad", [(i, i ^ 1) for i in range(bands)])
    changed = len(EDGE_CHANGED)
    whole = jax.ShapeDtypeStruct(state.shape, F32)
    settled, part = pl.pallas_call(
        main_kernel,
        out_shape=(whole, jax.ShapeDtypeStruct((changed, 2, height, width), F32)),
        in_specs=[VMEM],
        out_specs=(ANY, VMEM),
        scratch_shapes=[
            pltpu.VMEM((8, radii, height + 2 * ROWS, width), F32),
            pltpu.VMEM(state.shape, F32),
            pltpu.SemaphoreType.DMA((radii,)),
        ],
        compiler_params=GRANT,
        cost_estimate=pl.CostEstimate(flops=4000000000, bytes_accessed=4 * 2**20, transcendentals=0),
        name="main",
    )(remapped)
    relayed = pl.pallas_call(
        relay_kernel,
        out_shape=edge,
        in_specs=[VMEM, ANY],
        out_specs=VMEM,
        compiler_params=GRANT,
        name="relay",
    )(relayed, part)
    below = lax.ppermute(relayed, "rad", [(i + 2, i + 1) for i in odd])
    return pl.pallas_call(
        functools.partial(finish_kernel, radii),
        out_shape=whole,
        in_specs=[ANY, VMEM, VMEM, VMEM, VMEM, VMEM],
        out_specs=ANY,
        scratch_shapes=[
            pltpu.VMEM((2, changed, height, width), F32),
            pltpu.SemaphoreType.DMA((2, 2)),
        ],
        input_output_aliases={0: 0},
        compiler_params=GRANT,
        name="finish",
    )(settled, remapped, part, below, chip, above)


def solution(mesh):
    in_specs = (P(None, "rad", None, "az"), P("rad"), P("rad"))
    out_specs = P(None, "rad", None, "az")
    return jax.shard_map(
        on_device, mesh=mesh, in_specs=in_specs, out_specs=out_specs, check_vma=False
    )
```

```python
import functools

import jax
import jax.numpy as jnp
from jax import lax
from jax.experimental import pallas as pl
from jax.experimental.pallas import tpu as pltpu
from jax.sharding import PartitionSpec as P

F32 = jnp.float32
VMEM = pl.BlockSpec(memory_space=pltpu.VMEM)
SMEM = pl.BlockSpec(memory_space=pltpu.SMEM)
ANY = pl.BlockSpec(memory_space=pl.ANY)
GRANT = pltpu.CompilerParams(vmem_limit_bytes=16 * 2**20)
ROWS = 8
EDGE_FIELDS = (1, 2, 3, 6, 7)
SIDE_FIELDS = (0, 2, 4, 6, 7)
EDGE_CHANGED = (0, 1, 5, 6, 7)
EDGE_SETTLED = (2, 3, 4)


def remap_kernel(shifts_ref, fracs_ref, x_ref, o_ref, ends_ref):
    blocks, height, width = x_ref.shape
    tall = height + 1
    mine = lax.rem(lax.axis_index("az"), shifts_ref.shape[0])
    shift = shifts_ref[mine]
    frac = fracs_ref[mine]
    block_shift = lax.div(shift, width)
    lane_shift = lax.rem(shift, width)
    next_shift = lax.rem(lane_shift + 1, width)
    lane = lax.broadcasted_iota(jnp.int32, (height, width), 1)
    own = lane + lane_shift < width
    own_next = lane + lane_shift + 1 < width
    for i in range(blocks):
        near = x_ref[lax.rem(i - block_shift + blocks, blocks)]
        far = x_ref[lax.rem(i - block_shift - 1 + 2 * blocks, blocks)]
        first = pltpu.roll(jnp.where(own, near, far), lane_shift, 1)
        second = pltpu.roll(jnp.where(own_next, near, far), next_shift, 1)
        o_ref[tall * i : tall * i + height, :] = (1.0 - frac) * first + frac * second
    pair = lax.shift_right_logical(lane, 1)
    ends = jnp.zeros((height, width), F32)
    for i in range(blocks):
        cells = o_ref[tall * i : tall * i + height, :]
        ends = jnp.where(pair == i, pltpu.roll(cells, (2 * i + 1) % width, 1), ends)
    rows = jnp.transpose(jnp.concatenate([ends, jnp.zeros((width - height, width), F32)], axis=0))
    used = 2 * blocks
    ends_ref[0] = rows[:used]
    ends_ref[1] = pltpu.roll(rows[:used], height, 1)
    for i in range(blocks):
        last = 2 * ((i - 1) % blocks)
        head = 2 * ((i + 1) % blocks) + 1
        at = tall * i + height
        o_ref[at : at + 1, :] = ends_ref[0, last : last + 1, :] + ends_ref[1, head : head + 1, :]


def slab(s_ref, at, height):
    return s_ref[at * (height + 1) : at * (height + 1) + height]


def products(S):
    rho, vx, vy, vz, bx, by, bz, ent = S
    return (
        vy * bz - vz * by,
        vz * bx - vx * bz,
        vx * by - vy * bx,
        rho * vx,
        rho * vy,
        rho * vz,
        ent,
        0.5 * (bx * bx + by * by + bz * bz),
    )


def edge_kernel(radii, s_ref, far_ref, chip_ref):
    height = far_ref.shape[1]
    odd = lax.rem(lax.axis_index("rad"), 2) == 1
    low = products([slab(s_ref, v * radii, height) for v in range(8)])
    high = products([slab(s_ref, v * radii + radii - 1, height) for v in range(8)])
    for at, field in enumerate(EDGE_FIELDS):
        far_ref[at] = jnp.where(odd, high[field], low[field])
        chip_ref[at] = jnp.where(odd, low[field], high[field])


def main_kernel(s_ref, o_ref, part_ref, f_ref, done_ref, sems):
    variables, radii, height, width = done_ref.shape
    bands = lax.axis_size("rad")
    band = lax.axis_index("rad")
    total_radii = radii * bands
    pad = ROWS
    tall = height + 1
    side = lax.broadcasted_iota(jnp.int32, (ROWS, width), 1)
    spot = lax.broadcasted_iota(jnp.int32, (ROWS, width), 0) + jnp.where(side == 0, 0, height)
    lane = lax.broadcasted_iota(jnp.int32, (height, width), 1)
    level = lax.broadcasted_iota(jnp.int32, (height, width), 0)
    zk = (level.astype(F32) + 0.5) / height - 0.5
    for r in range(radii):
        for at, field in enumerate(products([slab(s_ref, v * radii + r, height) for v in range(8)])):
            f_ref[at, r, pad : pad + height] = field
            f_ref[at, r, :pad] = jnp.zeros((pad, width), F32)
            f_ref[at, r, pad + height :] = jnp.zeros((pad, width), F32)
    copies = []
    for r in (1, 2, 0, 3):
        rho, vx, vy, vz, bx, by, bz, ent = [slab(s_ref, v * radii + r, height) for v in range(8)]
        tails = products([s_ref[(v * radii + r) * tall + height : (v * radii + r + 1) * tall] for v in range(8)])
        xr = ((band * radii + r).astype(F32) + 0.5) / total_radii - 0.5
        outer = r == 0 or r == radii - 1

        def dx(at):
            if r == 0:
                return 0.5 * f_ref[at, 1, pad : pad + height]
            minus = f_ref[at, r - 1, pad : pad + height]
            if r == radii - 1:
                return -0.5 * minus
            return 0.5 * (f_ref[at, r + 1, pad : pad + height] - minus)

        def dy(at):
            here = f_ref[at, r, pad : pad + height]
            row = jnp.broadcast_to(tails[at], (ROWS, width))
            next_to = jnp.concatenate(
                [
                    jnp.take_along_axis(row, spot + k * ROWS, axis=1, mode="promise_in_bounds")
                    for k in range(height // ROWS)
                ],
                axis=0,
            )
            plus = jnp.where(lane == width - 1, next_to, pltpu.roll(here, width - 1, 1))
            minus = jnp.where(lane == 0, next_to, pltpu.roll(here, 1, 1))
            return 0.5 * (plus - minus)

        def dz(at):
            plus = f_ref[at, r, pad + 1 : pad + 1 + height]
            minus = f_ref[at, r, pad - 1 : pad - 1 + height]
            return 0.5 * (plus - minus)

        new = (
            rho + 0.2 * -(dx(3) + dy(4) + dz(5)),
            vx + 0.2 * (2.0 * vy + 3.0 * xr - dx(7)),
            vy + 0.2 * (-0.5 * vx - dy(7)),
            vz + 0.2 * (-zk - dz(7)),
            bx + 0.2 * (dy(2) - dz(1)),
            by + 0.2 * (dz(0) - dx(2)),
            bz + 0.2 * (dx(1) - dy(0)),
            ent + 0.2 * -(vx * dx(6) + vy * dy(6) + vz * dz(6)),
        )
        for v in range(variables):
            if outer and v in EDGE_CHANGED:
                part_ref[EDGE_CHANGED.index(v), r // (radii - 1)] = new[v]
            else:
                done_ref[v, r] = new[v]
        span = slice(EDGE_SETTLED[0], EDGE_SETTLED[-1] + 1) if outer else slice(0, variables)
        copy = pltpu.make_async_copy(done_ref.at[span, r], o_ref.at[span, r], sems.at[r])
        copy.start()
        copies.append(copy)
    for copy in copies:
        copy.wait()


def add_halo(radii, outward, halo_refs, s_ref, part_ref, o_ref, done_ref, sems):
    height = done_ref.shape[1]
    odd = lax.rem(lax.axis_index("rad"), 2)
    pair = odd if outward else 1 - odd
    upper = pair == 1
    step = jnp.where(upper, 0.1, -0.1)
    below_ref, above_ref = halo_refs
    wy, wz, fx, es, pm = [
        step * (below_ref[at] if below_ref is above_ref else jnp.where(upper, above_ref[at], below_ref[at]))
        for at in range(len(EDGE_FIELDS))
    ]
    vx = jnp.where(upper, slab(s_ref, 2 * radii - 1, height), slab(s_ref, radii, height))
    changes = (-fx, -pm, -wz, wy, -(vx * es))
    copies = []
    for group, (begin, end) in enumerate(((0, 2), (2, 5))):
        for at in range(begin, end):
            done_ref[at] = part_ref[at, pair] + changes[at]
        first = EDGE_CHANGED[begin]
        copy = pltpu.make_async_copy(
            done_ref.at[begin:end],
            o_ref.at[first : first + end - begin, pair * (radii - 1)],
            sems.at[group],
        )
        copy.start()
        copies.append(copy)
    for copy in copies:
        copy.wait()


def relay_kernel(radii, from_ref, base_ref, s_ref, part_ref, chip_ref, to_ref, o_ref, done_ref, sems):
    del base_ref
    to_ref[...] = from_ref[...]
    add_halo(radii, False, (chip_ref, chip_ref), s_ref, part_ref, o_ref, done_ref, sems)


def finish_kernel(radii, base_ref, s_ref, part_ref, below_ref, above_ref, o_ref, done_ref, sems):
    del base_ref
    add_halo(radii, True, (below_ref, above_ref), s_ref, part_ref, o_ref, done_ref, sems)


def on_device(state, shifts, fracs):
    variables, radii, height, width = state.shape
    count = variables * radii
    bands = lax.axis_size("rad")
    turned = lax.all_to_all(state.reshape(count, height, width), "az", 0, 0, tiled=True)
    moved = pl.pallas_call(
        remap_kernel,
        out_shape=jax.ShapeDtypeStruct((count * (height + 1), width), F32),
        in_specs=[SMEM, SMEM, VMEM],
        out_specs=VMEM,
        scratch_shapes=[pltpu.VMEM((2, 2 * count, width), F32)],
        compiler_params=GRANT,
        name="remap",
    )(shifts, fracs, turned)
    moved = moved.reshape(count, height + 1, 1, width)
    remapped = lax.all_to_all(moved, "az", 0, 0, tiled=True).reshape(count * (height + 1), width)
    edge = jax.ShapeDtypeStruct((len(EDGE_FIELDS), height, width), F32)
    far, chip = pl.pallas_call(
        functools.partial(edge_kernel, radii),
        out_shape=(edge, edge),
        in_specs=[VMEM],
        out_specs=(VMEM, VMEM),
        compiler_params=GRANT,
        name="edges",
    )(remapped)
    odd = range(1, bands - 1, 2)
    relayed = lax.ppermute(far, "rad", [(i, i + 2) for i in odd])
    above = lax.ppermute(far, "rad", [(i + 1, i) for i in odd])
    chip = lax.ppermute(chip, "rad", [(i, i ^ 1) for i in range(bands)])
    changed = len(EDGE_CHANGED)
    whole = jax.ShapeDtypeStruct(state.shape, F32)
    settled, part = pl.pallas_call(
        main_kernel,
        out_shape=(whole, jax.ShapeDtypeStruct((changed, 2, height, width), F32)),
        in_specs=[VMEM],
        out_specs=(ANY, VMEM),
        scratch_shapes=[
            pltpu.VMEM((8, radii, height + 2 * ROWS, width), F32),
            pltpu.VMEM(state.shape, F32),
            pltpu.SemaphoreType.DMA((radii,)),
        ],
        compiler_params=GRANT,
        cost_estimate=pl.CostEstimate(flops=4000000000, bytes_accessed=4 * 2**20, transcendentals=0),
        name="main",
    )(remapped)
    scratch = [pltpu.VMEM((changed, height, width), F32), pltpu.SemaphoreType.DMA((2,))]
    relayed, settled = pl.pallas_call(
        functools.partial(relay_kernel, radii),
        out_shape=(edge, whole),
        in_specs=[VMEM, ANY, VMEM, VMEM, VMEM],
        out_specs=(VMEM, ANY),
        scratch_shapes=scratch,
        input_output_aliases={1: 1},
        compiler_params=GRANT,
        name="relay",
    )(relayed, settled, remapped, part, chip)
    below = lax.ppermute(relayed, "rad", [(i + 2, i + 1) for i in odd])
    return pl.pallas_call(
        functools.partial(finish_kernel, radii),
        out_shape=whole,
        in_specs=[ANY, VMEM, VMEM, VMEM, VMEM],
        out_specs=ANY,
        scratch_shapes=scratch,
        input_output_aliases={0: 0},
        compiler_params=GRANT,
        name="finish",
    )(settled, remapped, part, below, above)


def solution(mesh):
    in_specs = (P(None, "rad", None, "az"), P("rad"), P("rad"))
    out_specs = P(None, "rad", None, "az")
    return jax.shard_map(
        on_device, mesh=mesh, in_specs=in_specs, out_specs=out_specs, check_vma=False
    )
```

```python
import functools

import jax
import jax.numpy as jnp
from jax import lax
from jax.experimental import pallas as pl
from jax.experimental.pallas import tpu as pltpu
from jax.sharding import PartitionSpec as P

F32 = jnp.float32
VMEM = pl.BlockSpec(memory_space=pltpu.VMEM)
SMEM = pl.BlockSpec(memory_space=pltpu.SMEM)
ANY = pl.BlockSpec(memory_space=pl.ANY)
GRANT = pltpu.CompilerParams(vmem_limit_bytes=16 * 2**20)
ROWS = 8
EDGE_FIELDS = (1, 2, 3, 6, 7)
SIDE_FIELDS = (0, 2, 4, 6, 7)
EDGE_CHANGED = (0, 1, 5, 6, 7)
EDGE_SETTLED = (2, 3, 4)


def remap_kernel(shifts_ref, fracs_ref, x_ref, o_ref):
    blocks, height, width = x_ref.shape
    tall = height + 1
    mine = lax.rem(lax.axis_index("az"), shifts_ref.shape[0])
    shift = shifts_ref[mine]
    frac = fracs_ref[mine]
    block_shift = lax.div(shift, width)
    lane_shift = lax.rem(shift, width)
    next_shift = lax.rem(lane_shift + 1, width)
    lane = lax.broadcasted_iota(jnp.int32, (height, width), 1)
    own = lane + lane_shift < width
    own_next = lane + lane_shift + 1 < width
    for i in range(blocks):
        near = x_ref[lax.rem(i - block_shift + blocks, blocks)]
        far = x_ref[lax.rem(i - block_shift - 1 + 2 * blocks, blocks)]
        first = pltpu.roll(jnp.where(own, near, far), lane_shift, 1)
        second = pltpu.roll(jnp.where(own_next, near, far), next_shift, 1)
        o_ref[tall * i : tall * i + height, :] = (1.0 - frac) * first + frac * second
    pair = lax.shift_right_logical(lane, 1)
    ends = jnp.zeros((height, width), F32)
    for i in range(blocks):
        cells = o_ref[tall * i : tall * i + height, :]
        ends = jnp.where(pair == i, pltpu.roll(cells, (2 * i + 1) % width, 1), ends)
    tip = 2 * (blocks - 1)
    before = jnp.where(lane == 0, pltpu.roll(ends, width - tip, 1), pltpu.roll(ends, 2, 1))
    after = jnp.where(lane == tip, pltpu.roll(ends, tip - 1, 1), pltpu.roll(ends, width - 3, 1))
    rows = jnp.transpose(jnp.concatenate([before, after], axis=0))
    for i in range(blocks):
        at = tall * i + height
        o_ref[at : at + 1, :] = rows[2 * i : 2 * i + 1]


def slab(s_ref, at, height):
    return s_ref[at * (height + 1) : at * (height + 1) + height]


def products(S):
    rho, vx, vy, vz, bx, by, bz, ent = S
    return (
        vy * bz - vz * by,
        vz * bx - vx * bz,
        vx * by - vy * bx,
        rho * vx,
        rho * vy,
        rho * vz,
        ent,
        0.5 * (bx * bx + by * by + bz * bz),
    )


def edge_kernel(radii, s_ref, far_ref, chip_ref):
    height = far_ref.shape[1]
    odd = lax.rem(lax.axis_index("rad"), 2) == 1
    low = products([slab(s_ref, v * radii, height) for v in range(8)])
    high = products([slab(s_ref, v * radii + radii - 1, height) for v in range(8)])
    for at, field in enumerate(EDGE_FIELDS):
        far_ref[at] = jnp.where(odd, high[field], low[field])
        chip_ref[at] = jnp.where(odd, low[field], high[field])


def main_kernel(s_ref, o_ref, part_ref, f_ref, done_ref, sems):
    variables, radii, height, width = done_ref.shape
    bands = lax.axis_size("rad")
    band = lax.axis_index("rad")
    total_radii = radii * bands
    pad = ROWS
    tall = height + 1
    side = lax.broadcasted_iota(jnp.int32, (ROWS, width), 1)
    spot = lax.broadcasted_iota(jnp.int32, (ROWS, width), 0) + jnp.where(side == 0, 0, height)
    lane = lax.broadcasted_iota(jnp.int32, (height, width), 1)
    level = lax.broadcasted_iota(jnp.int32, (height, width), 0)
    zk = (level.astype(F32) + 0.5) / height - 0.5
    for r in range(radii):
        for at, field in enumerate(products([slab(s_ref, v * radii + r, height) for v in range(8)])):
            f_ref[at, r, pad : pad + height] = field
            f_ref[at, r, :pad] = jnp.zeros((pad, width), F32)
            f_ref[at, r, pad + height :] = jnp.zeros((pad, width), F32)
    copies = []
    for r in (1, 2, 0, 3):
        rho, vx, vy, vz, bx, by, bz, ent = [slab(s_ref, v * radii + r, height) for v in range(8)]
        tails = products([s_ref[(v * radii + r) * tall + height : (v * radii + r + 1) * tall] for v in range(8)])
        xr = ((band * radii + r).astype(F32) + 0.5) / total_radii - 0.5
        outer = r == 0 or r == radii - 1

        def dx(at):
            if r == 0:
                return 0.5 * f_ref[at, 1, pad : pad + height]
            minus = f_ref[at, r - 1, pad : pad + height]
            if r == radii - 1:
                return -0.5 * minus
            return 0.5 * (f_ref[at, r + 1, pad : pad + height] - minus)

        def dy(at):
            here = f_ref[at, r, pad : pad + height]
            row = jnp.broadcast_to(tails[at], (ROWS, width))
            next_to = jnp.concatenate(
                [
                    jnp.take_along_axis(row, spot + k * ROWS, axis=1, mode="promise_in_bounds")
                    for k in range(height // ROWS)
                ],
                axis=0,
            )
            plus = jnp.where(lane == width - 1, next_to, pltpu.roll(here, width - 1, 1))
            minus = jnp.where(lane == 0, next_to, pltpu.roll(here, 1, 1))
            return 0.5 * (plus - minus)

        def dz(at):
            plus = f_ref[at, r, pad + 1 : pad + 1 + height]
            minus = f_ref[at, r, pad - 1 : pad - 1 + height]
            return 0.5 * (plus - minus)

        new = (
            rho + 0.2 * -(dx(3) + dy(4) + dz(5)),
            vx + 0.2 * (2.0 * vy + 3.0 * xr - dx(7)),
            vy + 0.2 * (-0.5 * vx - dy(7)),
            vz + 0.2 * (-zk - dz(7)),
            bx + 0.2 * (dy(2) - dz(1)),
            by + 0.2 * (dz(0) - dx(2)),
            bz + 0.2 * (dx(1) - dy(0)),
            ent + 0.2 * -(vx * dx(6) + vy * dy(6) + vz * dz(6)),
        )
        for v in range(variables):
            if outer and v in EDGE_CHANGED:
                part_ref[EDGE_CHANGED.index(v), r // (radii - 1)] = new[v]
            else:
                done_ref[v, r] = new[v]
        span = slice(EDGE_SETTLED[0], EDGE_SETTLED[-1] + 1) if outer else slice(0, variables)
        copy = pltpu.make_async_copy(done_ref.at[span, r], o_ref.at[span, r], sems.at[r])
        copy.start()
        copies.append(copy)
    for copy in copies:
        copy.wait()


def relay_kernel(from_ref, part_ref, to_ref):
    del part_ref
    to_ref[...] = from_ref[...]


def finish_kernel(radii, base_ref, s_ref, part_ref, below_ref, chip_ref, above_ref, o_ref, done_ref, sems):
    del base_ref
    height = chip_ref.shape[1]
    odd = lax.rem(lax.axis_index("rad"), 2) == 1
    copies = []
    for pair in range(2):
        r = pair * (radii - 1)
        step = 0.1 if pair else -0.1
        halo = []
        for at in range(len(EDGE_FIELDS)):
            outside = above_ref[at] if pair else below_ref[at]
            far_here = odd if pair else jnp.logical_not(odd)
            halo.append(step * jnp.where(far_here, outside, chip_ref[at]))
        wy, wz, fx, es, pm = halo
        vx = slab(s_ref, radii + r, height)
        changes = (-fx, -pm, -wz, wy, -(vx * es))
        for group, (begin, end) in enumerate(((0, 2), (2, 5))):
            for at in range(begin, end):
                done_ref[pair, at] = part_ref[at, pair] + changes[at]
            first = EDGE_CHANGED[begin]
            copy = pltpu.make_async_copy(
                done_ref.at[pair, begin:end],
                o_ref.at[first : first + end - begin, r],
                sems.at[group, pair],
            )
            copy.start()
            copies.append(copy)
    for copy in copies:
        copy.wait()


def on_device(state, shifts, fracs):
    variables, radii, height, width = state.shape
    count = variables * radii
    bands = lax.axis_size("rad")
    turned = lax.all_to_all(state.reshape(count, height, width), "az", 0, 0, tiled=True)
    moved = pl.pallas_call(
        remap_kernel,
        out_shape=jax.ShapeDtypeStruct((count * (height + 1), width), F32),
        in_specs=[SMEM, SMEM, VMEM],
        out_specs=VMEM,
        compiler_params=GRANT,
        name="remap",
    )(shifts, fracs, turned)
    moved = moved.reshape(count, height + 1, 1, width)
    remapped = lax.all_to_all(moved, "az", 0, 0, tiled=True).reshape(count * (height + 1), width)
    edge = jax.ShapeDtypeStruct((len(EDGE_FIELDS), height, width), F32)
    far, chip = pl.pallas_call(
        functools.partial(edge_kernel, radii),
        out_shape=(edge, edge),
        in_specs=[VMEM],
        out_specs=(VMEM, VMEM),
        compiler_params=GRANT,
        name="edges",
    )(remapped)
    odd = range(1, bands - 1, 2)
    relayed = lax.ppermute(far, "rad", [(i, i + 2) for i in odd])
    above = lax.ppermute(far, "rad", [(i + 1, i) for i in odd])
    chip = lax.ppermute(chip, "rad", [(i, i ^ 1) for i in range(bands)])
    changed = len(EDGE_CHANGED)
    whole = jax.ShapeDtypeStruct(state.shape, F32)
    settled, part = pl.pallas_call(
        main_kernel,
        out_shape=(whole, jax.ShapeDtypeStruct((changed, 2, height, width), F32)),
        in_specs=[VMEM],
        out_specs=(ANY, VMEM),
        scratch_shapes=[
            pltpu.VMEM((8, radii, height + 2 * ROWS, width), F32),
            pltpu.VMEM(state.shape, F32),
            pltpu.SemaphoreType.DMA((radii,)),
        ],
        compiler_params=GRANT,
        cost_estimate=pl.CostEstimate(flops=4000000000, bytes_accessed=4 * 2**20, transcendentals=0),
        name="main",
    )(remapped)
    relayed = pl.pallas_call(
        relay_kernel,
        out_shape=edge,
        in_specs=[VMEM, ANY],
        out_specs=VMEM,
        compiler_params=GRANT,
        name="relay",
    )(relayed, part)
    below = lax.ppermute(relayed, "rad", [(i + 2, i + 1) for i in odd])
    return pl.pallas_call(
        functools.partial(finish_kernel, radii),
        out_shape=whole,
        in_specs=[ANY, VMEM, VMEM, VMEM, VMEM, VMEM],
        out_specs=ANY,
        scratch_shapes=[
            pltpu.VMEM((2, changed, height, width), F32),
            pltpu.SemaphoreType.DMA((2, 2)),
        ],
        input_output_aliases={0: 0},
        compiler_params=GRANT,
        name="finish",
    )(settled, remapped, part, below, chip, above)


def solution(mesh):
    in_specs = (P(None, "rad", None, "az"), P("rad"), P("rad"))
    out_specs = P(None, "rad", None, "az")
    return jax.shard_map(
        on_device, mesh=mesh, in_specs=in_specs, out_specs=out_specs, check_vma=False
    )
```
